32 devices in a mesh: groups: 2 (over y), term: 4 (over z), sector: 4 (over x, core).
Axes of the slice: x: 2, y: 2, z: 4, core: 2. Of those that a mesh axis runs over, the one named last changes fastest.
Arguments:
- wave_blocks: bfloat16 [8, 512, 512], P(('groups', 'sector')), parts along dimension 0, may hold values from -6 to 6
- sector_rows: int32 [8], P(('groups', 'sector')), parts along dimension 0, may hold values from 64 to 512, as said below
- term_class: int32 [32], P(('groups', 'term')), parts along dimension 0, may hold values from 0 to 4, as said below
- left_env: bfloat16 [32, 4, 512, 512], P(('groups', 'term'), 'sector'), parts along dimension 0, may hold values from -0.25 to 0.25
- right_env: bfloat16 [32, 4, 512, 512], P(('groups', 'term'), 'sector'), parts along dimension 0, may hold values from -0.0625 to 0.0625
Outputs:
- applied: bfloat16 [8, 512, 512], P(('groups', 'sector'), 'term'), parts along dimension 0
The draws below stay inside these ranges and needn't reach their ends.
There are 2 independent parts, one for each index of `groups`. The reference program is written for one: setup_inputs(seed, part) draws one part's arguments, and reference() takes and returns one part's arrays. A program takes and returns all parts, laid end to end along the dimension named above; each array names one. Nothing has to cross between parts.
Inputs may be any that keep to these rules, and one draw needn't show every extreme that they name: `sector_rows`: some sector has all 512 rows live in every draw. `term_class`: each of the five classes is held by at least one term.
All inputs are finite; a program needn't handle non-finite values.
Results may differ from the reference program's by a relative error of at most 0.0049.
Values may be sent and summed in bfloat16 or wider, within the bound.
No kernel may reach another device: no remote copies, remote signals or barrier semaphores. Data moves between devices by JAX's collectives and lax.ppermute only.
A program may use at most 64 MiB of HBM per device.

```python
import jax
import jax.numpy as jnp
from jax import lax

PAD = 512
TERMS = 16
SECTORS = 4
GRID = 2


def draw_sector_rows(key, part):
    key = jax.random.fold_in(key, 11)
    first, second = jax.random.split(key)
    values = jax.random.randint(first, (SECTORS,), PAD // 8, PAD + 1)
    position = jax.random.randint(second, (), 0, SECTORS)
    return jnp.where(jnp.arange(SECTORS) == position, PAD, values).astype(jnp.int32)


def draw_term_class(key, part):
    key = jax.random.fold_in(key, 23)
    order = jax.random.permutation(key, TERMS)
    return (order % 5).astype(jnp.int32)


def steps_of(own_key, shape, cuts, low, top_value):
    level, own = 1.0, jax.random.fold_in(own_key, 6)
    for dim, blocks in cuts:
        heights = jnp.exp(jax.random.uniform(jax.random.fold_in(own, dim), (blocks,), jnp.float32, low / len(cuts), top_value / len(cuts)))
        level = level * jnp.repeat(heights, shape[dim] // blocks).reshape([-1 if axis == dim else 1 for axis in range(len(shape))])
    return level


def normal_values(stream_key, shape, scale, most, cuts=(), kind=jnp.bfloat16):
    result = jax.random.normal(stream_key, shape, jnp.float32) * scale
    if len(cuts) > 0:
        result = steps_of(stream_key, shape, cuts, -0.22, 0.18) * result
    return jnp.clip(result, min=-most, max=most).astype(kind)


def setup_inputs(seed: int = 0, part: int = 0) -> dict:
    arg_keys = jax.random.split(jax.random.key(seed), 6)
    part_splits = jax.random.split(jax.random.fold_in(arg_keys[5], part), 6)
    wave_blocks = normal_values(part_splits[0], (SECTORS, PAD, PAD), 1.0, 6.0, ((0, 4),))
    sector_rows = draw_sector_rows(jax.random.fold_in(jax.random.fold_in(arg_keys[5], part), 71), part)
    term_class = draw_term_class(jax.random.fold_in(jax.random.fold_in(arg_keys[5], part), 71), part)
    left_env = normal_values(part_splits[3], (TERMS, SECTORS, PAD, PAD), PAD ** -0.5, 0.25, ((0, 4), (1, 4)))
    right_env = normal_values(part_splits[4], (TERMS, SECTORS, PAD, PAD), (TERMS * PAD) ** -0.5, 0.0625, ((0, 4), (1, 4)))
    return dict(wave_blocks=wave_blocks, sector_rows=sector_rows, term_class=term_class, left_env=left_env, right_env=right_env)


def reference(wave_blocks, sector_rows, term_class, left_env, right_env):
    row_index = jnp.arange(PAD, dtype=jnp.int32)
    masked = jnp.where(row_index[None, :, None] < sector_rows[:, None, None], wave_blocks, jnp.zeros((), wave_blocks.dtype))
    offset_table = jnp.array([0, 1, -1, GRID, -GRID], dtype=jnp.int32)
    offsets = offset_table[term_class]

    def one_block(block):
        source = block - offsets
        usable = (source >= 0) & (source < SECTORS)
        usable = usable & jnp.logical_not((term_class == 1) & (block % GRID == 0))
        usable = usable & jnp.logical_not((term_class == 2) & (block % GRID == GRID - 1))
        clipped = jnp.clip(source, 0, SECTORS - 1).astype(jnp.int32)
        picked = jnp.where(usable[:, None, None], masked[clipped], jnp.zeros((), masked.dtype))
        lefts = lax.dynamic_index_in_dim(left_env, block, 1, keepdims=False)
        rights = lax.dynamic_index_in_dim(right_env, block, 1, keepdims=False)
        halfway = jnp.einsum('kij,kjc->kic', lefts.astype(jnp.float32), picked.astype(jnp.float32)).astype(jnp.bfloat16)
        summed = jnp.einsum('kic,kdc->id', halfway.astype(jnp.float32), rights.astype(jnp.float32))
        kept = row_index[:, None] < sector_rows[block]
        return jnp.where(kept, summed, jnp.zeros((), summed.dtype)).astype(jnp.bfloat16)

    return lax.map(one_block, jnp.arange(SECTORS, dtype=jnp.int32))
```

```python
import functools

import jax
import jax.numpy as jnp
from jax import lax
from jax.experimental import pallas as pl
from jax.experimental.pallas import tpu as pltpu
from jax.sharding import PartitionSpec as P

SMEM = pl.BlockSpec(memory_space=pltpu.SMEM)
VMEM = pl.BlockSpec(memory_space=pltpu.VMEM)


def neighbour_moves(sectors, grid):
    down_in = [(s, s + 1) for s in range(sectors - 1) if (s + 1) % grid != 0]
    down_out = [(s, s - 1) for s in range(1, sectors) if s % grid != 0]
    up_in = [(s, s + grid) for s in range(sectors - grid)]
    up_out = [(s, s - grid) for s in range(grid, sectors)]
    moves = []
    for first, second in ((down_in, down_out), (up_in, up_out)):
        targets = [t for _, t in first + second]
        if len(set(targets)) == len(targets):
            moves.append([first + second])
        else:
            moves.append([first, second])
    return moves


def usable_of(kind, own, sectors, grid):
    column = lax.rem(own, grid)
    usable = kind == 0
    usable = usable | ((kind == 1) & (column != 0))
    usable = usable | ((kind == 2) & (column != grid - 1))
    usable = usable | ((kind == 3) & (own >= grid))
    return usable | ((kind == 4) & (own < sectors - grid))


def add_terms(classes, rows_refs, block_refs, slots, left, right, masked, total, sectors, grid):
    own = lax.axis_index("sector")
    pad = total.shape[0]
    row = lax.broadcasted_iota(jnp.int32, (pad, pad), 0)
    for place, (rows_ref, block_ref) in enumerate(zip(rows_refs, block_refs)):
        masked[place] = jnp.where(row < rows_ref[0], block_ref[0], jnp.zeros((), jnp.bfloat16))
    for term in range(left.shape[0]):
        kind = classes[term]
        member = functools.reduce(jnp.logical_or, [kind == k for k in slots])
        slot = sum(jnp.where(kind == k, place, 0) for k, place in slots.items())

        @pl.when(member & usable_of(kind, own, sectors, grid))
        def _():
            half = jnp.dot(left[term, 0], masked[slot], preferred_element_type=jnp.float32)
            total[...] += lax.dot_general(
                half.astype(jnp.bfloat16),
                right[term, 0],
                (((1,), (1,)), ((), ())),
                preferred_element_type=jnp.float32,
            )


def first_kernel(slots, count, sectors, grid, classes, *refs):
    rows_refs, block_refs = refs[:count], refs[count : 2 * count]
    left, right, total, masked = refs[2 * count :]
    total[...] = jnp.zeros_like(total)
    add_terms(classes, rows_refs, block_refs, slots, left, right, masked, total, sectors, grid)


def second_kernel(slots, count, sectors, grid, classes, *refs):
    rows_refs, block_refs = refs[:count], refs[count : 2 * count]
    left, right, before, kept = refs[2 * count : 2 * count + 4]
    sent = refs[2 * count + 4 : -2]
    masked, total = refs[-2:]
    total[...] = before[...]
    add_terms(classes, rows_refs, block_refs, slots, left, right, masked, total, sectors, grid)
    share = kept.shape[0]
    parts = len(sent) + 1
    me = lax.axis_index("term")
    kept[...] = total[pl.ds(pl.multiple_of(me * share, share), share), :]
    for step in range(1, parts):
        to = lax.rem(me + step, parts)
        sent[step - 1][...] = total[pl.ds(pl.multiple_of(to * share, share), share), :].astype(jnp.bfloat16)


def last_kernel(rows_ref, kept, *refs):
    got, out = refs[:-1], refs[-1]
    share = kept.shape[0]
    total = kept[...]
    for part in got:
        total = total + part[...].astype(jnp.float32)
    row = lax.axis_index("term") * share + lax.broadcasted_iota(jnp.int32, total.shape, 0)
    out[0] = jnp.where(row < rows_ref[0], total, 0.0).astype(jnp.bfloat16)


def per_device(wave_blocks, sector_rows, term_class, left_env, right_env):
    pad = wave_blocks.shape[1]
    sectors, parts = lax.axis_size("sector"), lax.axis_size("term")
    grid = max(2, sectors // 4)
    share = pad // parts
    down, up = neighbour_moves(sectors, grid)
    send = lambda array, pairs: lax.ppermute(array, "sector", pairs)
    down_blocks = [send(wave_blocks, pairs) for pairs in down]
    up_blocks = [send(wave_blocks, pairs) for pairs in up]
    down_rows = [send(sector_rows, pairs) for pairs in down]
    up_rows = [send(sector_rows, pairs) for pairs in up]
    limit = pltpu.CompilerParams(vmem_limit_bytes=24 * 2**20)

    first = [wave_blocks] + down_blocks
    count = len(first)
    total = pl.pallas_call(
        functools.partial(first_kernel, {0: 0, 1: 1, 2: len(down)}, count, sectors, grid),
        out_shape=jax.ShapeDtypeStruct((pad, pad), jnp.float32),
        in_specs=[SMEM] * (1 + count) + [VMEM] * (count + 2),
        out_specs=VMEM,
        scratch_shapes=[pltpu.VMEM((count, pad, pad), jnp.bfloat16)],
        compiler_params=limit,
        name="near_terms",
    )(term_class, sector_rows, *down_rows, *first, left_env, right_env)

    count = len(up_blocks)
    kept, *sent = pl.pallas_call(
        functools.partial(second_kernel, {3: 0, 4: len(up) - 1}, count, sectors, grid),
        out_shape=[jax.ShapeDtypeStruct((share, pad), jnp.float32)]
        + [jax.ShapeDtypeStruct((share, pad), jnp.bfloat16)] * (parts - 1),
        in_specs=[SMEM] * (1 + count) + [VMEM] * (count + 3),
        out_specs=[VMEM] * parts,
        scratch_shapes=[pltpu.VMEM((count, pad, pad), jnp.bfloat16), pltpu.VMEM((pad, pad), jnp.float32)],
        compiler_params=limit,
        name="far_terms",
    )(term_class, *up_rows, *up_blocks, left_env, right_env, total)

    got = [
        lax.ppermute(part, "term", [(i, (i + step) % parts) for i in range(parts)])
        for step, part in enumerate(sent, 1)
    ]
    return pl.pallas_call(
        last_kernel,
        out_shape=jax.ShapeDtypeStruct((1, share, pad), jnp.bfloat16),
        in_specs=[SMEM] + [VMEM] * parts,
        out_specs=VMEM,
        compiler_params=limit,
        name="sum_parts",
    )(sector_rows, kept, *got)


def solution(mesh):
    placed = (
        P(("groups", "sector"), None, None),
        P(("groups", "sector")),
        P(("groups", "term")),
        P(("groups", "term"), "sector", None, None),
        P(("groups", "term"), "sector", None, None),
    )
    return jax.shard_map(
        per_device,
        mesh=mesh,
        in_specs=placed,
        out_specs=P(("groups", "sector"), "term", None),
        check_vma=False,
    )
```

```python
import functools

import jax
import jax.numpy as jnp
from jax import lax
from jax.experimental import pallas as pl
from jax.experimental.pallas import tpu as pltpu
from jax.sharding import PartitionSpec as P

SMEM = pl.BlockSpec(memory_space=pltpu.SMEM)
VMEM = pl.BlockSpec(memory_space=pltpu.VMEM)
HBM = pl.BlockSpec(memory_space=pltpu.HBM)


def neighbour_moves(sectors, grid):
    down_in = [(s, s + 1) for s in range(sectors - 1) if (s + 1) % grid != 0]
    down_out = [(s, s - 1) for s in range(1, sectors) if s % grid != 0]
    up_in = [(s, s + grid) for s in range(sectors - grid)]
    up_out = [(s, s - grid) for s in range(grid, sectors)]
    moves = []
    for first, second in ((down_in, down_out), (up_in, up_out)):
        targets = [t for _, t in first + second]
        if len(set(targets)) == len(targets):
            moves.append([first + second])
        else:
            moves.append([first, second])
    return moves


def usable_of(kind, own, sectors, grid):
    column = lax.rem(own, grid)
    usable = kind == 0
    usable = usable | ((kind == 1) & (column != 0))
    usable = usable | ((kind == 2) & (column != grid - 1))
    usable = usable | ((kind == 3) & (own >= grid))
    return usable | ((kind == 4) & (own < sectors - grid))


def slot_of(kind, slots):
    member = functools.reduce(jnp.logical_or, [kind == k for k in slots])
    return member, sum(jnp.where(kind == k, place, 0) for k, place in slots.items())


def mask_rows(block, rows):
    row = lax.broadcasted_iota(jnp.int32, block.shape, 0)
    return jnp.where(row < rows, block, jnp.zeros((), block.dtype))


def add_term(left, block, right, total):
    half = jnp.dot(left, block, preferred_element_type=jnp.float32)
    total[...] += lax.dot_general(
        half.astype(jnp.bfloat16), right, (((1,), (1,)), ((), ())), preferred_element_type=jnp.float32
    )


def near_kernel(slots, count, sectors, grid, classes_hbm, wave_hbm, left_hbm, right_hbm, *refs):
    rows_refs, block_refs, far_rows = refs[:count], refs[count : 2 * count - 1], refs[2 * count - 1 : -8]
    info, total, own_masked, lefts, rights, masked, classes, sems = refs[-8:]
    own = lax.axis_index("sector")
    terms = lefts.shape[0]
    get_classes = pltpu.make_async_copy(classes_hbm, classes, sems.at[0, terms])
    get_wave = pltpu.make_async_copy(wave_hbm, own_masked, sems.at[1, terms])
    get_classes.start()
    get_wave.start()
    copies = []
    for term in range(terms):
        get_left = pltpu.make_async_copy(left_hbm.at[term, 0], lefts.at[term], sems.at[0, term])
        get_right = pltpu.make_async_copy(right_hbm.at[term, 0], rights.at[term], sems.at[1, term])
        get_left.start()
        get_right.start()
        copies.append((get_left, get_right))
    for place, block_ref in enumerate(block_refs, 1):
        masked[place] = mask_rows(block_ref[0], rows_refs[place][0])
    total[...] = jnp.zeros_like(total)
    for place, rows_ref in enumerate(far_rows):
        info[terms + place] = rows_ref[0]
    get_classes.wait()
    for term in range(terms):
        info[term] = classes[term]
    get_wave.wait()
    masked[0] = mask_rows(own_masked[0], rows_refs[0][0])
    own_masked[0] = masked[0]
    for term in range(terms):
        for copy in copies[term]:
            copy.wait()
        member, slot = slot_of(classes[term], slots)

        @pl.when(member & usable_of(classes[term], own, sectors, grid))
        def _():
            add_term(lefts[term], masked[slot], rights[term], total)


def far_kernel(slots, count, sectors, grid, info, *refs):
    even_refs, odd_refs = refs[:count], refs[count : 2 * count]
    left, right, before, kept = refs[2 * count : 2 * count + 4]
    sent = refs[2 * count + 4 : -2]
    terms = left.shape[0]
    masked, total = refs[-2:]
    own = lax.axis_index("sector")
    even = lax.rem(own, 2) == 0
    for place in range(count):

        @pl.when(even)
        def _():
            masked[place] = mask_rows(even_refs[place][0], info[terms + place])

        @pl.when(jnp.logical_not(even))
        def _():
            masked[place] = mask_rows(odd_refs[place][0], info[terms + place])

    total[...] = before[...]
    for term in range(terms):
        member, slot = slot_of(info[term], slots)

        @pl.when(member & usable_of(info[term], own, sectors, grid))
        def _():
            add_term(left[term], masked[slot], right[term], total)

    share = kept.shape[0]
    parts = len(sent) + 1
    me = lax.axis_index("term")
    kept[...] = total[pl.ds(pl.multiple_of(me * share, share), share), :]
    for step in range(1, parts):
        to = lax.rem(me + step, parts)
        sent[step - 1][...] = total[pl.ds(pl.multiple_of(to * share, share), share), :].astype(jnp.bfloat16)


def last_kernel(rows_ref, kept, *refs):
    got, out = refs[:-1], refs[-1]
    share = kept.shape[0]
    total = kept[...]
    for part in got:
        total = total + part[...].astype(jnp.float32)
    row = lax.axis_index("term") * share + lax.broadcasted_iota(jnp.int32, total.shape, 0)
    out[0] = jnp.where(row < rows_ref[0], total, 0.0).astype(jnp.bfloat16)


def per_device(wave_blocks, sector_rows, term_class, left_env, right_env):
    pad = wave_blocks.shape[1]
    sectors, parts = lax.axis_size("sector"), lax.axis_size("term")
    grid = max(2, sectors // 4)
    share = pad // parts
    down, up = neighbour_moves(sectors, grid)
    send = lambda array, pairs: lax.ppermute(array, "sector", pairs)
    parity = lambda pairs, odd: [(s, t) for s, t in pairs if s % 2 == odd]
    even_blocks = [send(wave_blocks, parity(pairs, 0)) for pairs in up]
    down_blocks = [send(wave_blocks, pairs) for pairs in down]
    down_rows = [send(sector_rows, pairs) for pairs in down]
    up_rows = [send(sector_rows, pairs) for pairs in up]
    limit = pltpu.CompilerParams(vmem_limit_bytes=24 * 2**20)

    in_hbm = lambda array: pltpu.with_memory_space_constraint(array, pltpu.HBM)
    count = 1 + len(down_blocks)
    terms = left_env.shape[0]
    info, total, own_masked, lefts, rights = pl.pallas_call(
        functools.partial(near_kernel, {0: 0, 1: 1, 2: len(down)}, count, sectors, grid),
        out_shape=[
            jax.ShapeDtypeStruct((terms + len(up),), jnp.int32),
            jax.ShapeDtypeStruct((pad, pad), jnp.float32),
            jax.ShapeDtypeStruct((1, pad, pad), jnp.bfloat16),
            jax.ShapeDtypeStruct((terms, pad, pad), jnp.bfloat16),
            jax.ShapeDtypeStruct((terms, pad, pad), jnp.bfloat16),
        ],
        in_specs=[HBM] * 4 + [SMEM] * count + [VMEM] * (count - 1) + [SMEM] * len(up),
        out_specs=[SMEM] + [VMEM] * 4,
        scratch_shapes=[
            pltpu.VMEM((count, pad, pad), jnp.bfloat16),
            pltpu.SMEM((terms,), jnp.int32),
            pltpu.SemaphoreType.DMA((2, terms + 1)),
        ],
        compiler_params=limit,
        name="near_terms",
    )(*(in_hbm(a) for a in (term_class, wave_blocks, left_env, right_env)), sector_rows, *down_rows, *down_blocks, *up_rows)
    odd_blocks = [send(own_masked, parity(pairs, 1)) for pairs in up]

    count = len(up)
    kept, *sent = pl.pallas_call(
        functools.partial(far_kernel, {3: 0, 4: count - 1}, count, sectors, grid),
        out_shape=[jax.ShapeDtypeStruct((share, pad), jnp.float32)]
        + [jax.ShapeDtypeStruct((share, pad), jnp.bfloat16)] * (parts - 1),
        in_specs=[SMEM] + [VMEM] * (2 * count + 3),
        out_specs=[VMEM] * parts,
        scratch_shapes=[pltpu.VMEM((count, pad, pad), jnp.bfloat16), pltpu.VMEM((pad, pad), jnp.float32)],
        compiler_params=limit,
        name="far_terms",
    )(info, *even_blocks, *odd_blocks, lefts, rights, total)

    got = [
        lax.ppermute(part, "term", [(i, (i + step) % parts) for i in range(parts)])
        for step, part in enumerate(sent, 1)
    ]
    return pl.pallas_call(
        last_kernel,
        out_shape=jax.ShapeDtypeStruct((1, share, pad), jnp.bfloat16),
        in_specs=[SMEM] + [VMEM] * parts,
        out_specs=VMEM,
        compiler_params=limit,
        name="sum_parts",
    )(sector_rows, kept, *got)


def solution(mesh):
    placed = (
        P(("groups", "sector"), None, None),
        P(("groups", "sector")),
        P(("groups", "term")),
        P(("groups", "term"), "sector", None, None),
        P(("groups", "term"), "sector", None, None),
    )
    return jax.shard_map(
        per_device,
        mesh=mesh,
        in_specs=placed,
        out_specs=P(("groups", "sector"), "term", None),
        check_vma=False,
    )
```

```python
import functools

import jax
import jax.numpy as jnp
from jax import lax
from jax.experimental import pallas as pl
from jax.experimental.pallas import tpu as pltpu
from jax.sharding import PartitionSpec as P

SMEM = pl.BlockSpec(memory_space=pltpu.SMEM)
VMEM = pl.BlockSpec(memory_space=pltpu.VMEM)
HBM = pl.BlockSpec(memory_space=pltpu.HBM)
LIMIT = pltpu.CompilerParams(vmem_limit_bytes=24 * 2**20)


def neighbour_moves(sectors, grid):
    down_in = [(s, s + 1) for s in range(sectors - 1) if (s + 1) % grid != 0]
    down_out = [(s, s - 1) for s in range(1, sectors) if s % grid != 0]
    up_in = [(s, s + grid) for s in range(sectors - grid)]
    up_out = [(s, s - grid) for s in range(grid, sectors)]
    moves = []
    for first, second in ((down_in, down_out), (up_in, up_out)):
        targets = [t for _, t in first + second]
        if len(set(targets)) == len(targets):
            moves.append([first + second])
        else:
            moves.append([first, second])
    return moves


def usable_of(kind, own, sectors, grid):
    column = lax.rem(own, grid)
    usable = kind == 0
    usable = usable | ((kind == 1) & (column != 0))
    usable = usable | ((kind == 2) & (column != grid - 1))
    usable = usable | ((kind == 3) & (own >= grid))
    return usable | ((kind == 4) & (own < sectors - grid))


def slot_of(kind, slots):
    member = functools.reduce(jnp.logical_or, [kind == k for k in slots])
    return member, sum(jnp.where(kind == k, place, 0) for k, place in slots.items())


def shard_rows(shard, share):
    return pl.ds(pl.multiple_of(shard * share, share), share)


def add_terms(info, slots, sectors, grid, blocks, left, right, add):
    own = lax.axis_index("sector")
    for term in range(left.shape[0]):
        member, slot = slot_of(info[term], slots)
        usable = member & usable_of(info[term], own, sectors, grid)
        for place, block in enumerate(blocks):

            @pl.when(usable & (slot == place))
            def _():
                add(term, block)


def product(left, block, right):
    half = jnp.dot(left, block, preferred_element_type=jnp.float32)
    return lax.dot_general(
        half.astype(jnp.bfloat16), right, (((1,), (1,)), ((), ())), preferred_element_type=jnp.float32
    )


def mask_kernel(shared, classes_hbm, rows, wave_hbm, info, masked, first, rest, classes, sems):
    terms = classes.shape[0]
    copies = [
        pltpu.make_async_copy(wave_hbm, masked, sems.at[0]),
        pltpu.make_async_copy(classes_hbm, classes, sems.at[1]),
    ]
    for copy in copies:
        copy.start()
    for copy in copies:
        copy.wait()
    for term in range(terms):
        info[term] = classes[term]
    info[terms] = rows[0]
    row = lax.broadcasted_iota(jnp.int32, masked.shape[1:], 0)
    masked[0] = jnp.where(row < rows[0], masked[0], jnp.zeros((), jnp.bfloat16))
    odd = lax.rem(lax.axis_index("term"), 2)
    first[...] = masked[0, shard_rows(odd, shared), :]
    rest[...] = masked[0, pl.ds(2 * shared, rest.shape[0]), :]


def own_kernel(info, block, left_hbm, right_hbm, total, left, right, sems):
    copies = []
    for term in range(left.shape[0]):
        pair = (
            pltpu.make_async_copy(left_hbm.at[term, 0], left.at[term], sems.at[0, term]),
            pltpu.make_async_copy(right_hbm.at[term, 0], right.at[term], sems.at[1, term]),
        )
        for copy in pair:
            copy.start()
        copies.append(pair)
    total[...] = jnp.zeros_like(total)
    for term, pair in enumerate(copies):
        for copy in pair:
            copy.wait()

        @pl.when(info[term] == 0)
        def _():
            total[...] += product(left[term], block[0], right[term])


def near_kernel(slots, sectors, grid, info, *refs):
    blocks, (left, right, before, total) = refs[:-4], refs[-4:]
    total[...] = before[...]

    def add(term, block):
        total[...] += product(left[term], block[0], right[term])

    add_terms(info, slots, sectors, grid, blocks, left, right, add)


def far_first_kernel(slots, sectors, grid, count, info, *refs):
    firsts, swapped, rests = refs[:count], refs[count : 2 * count], refs[2 * count : 3 * count]
    left, right, before, sent, blocks, total = refs[3 * count :]
    me = lax.axis_index("term")
    odd = lax.rem(me, 2)
    partner = me + 1 - 2 * odd
    shared = firsts[0].shape[0]
    for place in range(count):
        blocks[place, shard_rows(odd, shared), :] = firsts[place][...]
        blocks[place, shard_rows(1 - odd, shared), :] = swapped[place][...]
        blocks[place, pl.ds(2 * shared, rests[place].shape[0]), :] = rests[place][...]
    passed, share = total.shape[0], total.shape[1]
    shards = [shard_rows(lax.rem(partner + 2 * (k + 1), 2 * (passed + 1)), share) for k in range(passed)]
    for k in range(passed):
        total[k] = before[shards[k], :]

    def add(term, block):
        for k in range(passed):
            total[k] += product(left[term, shards[k], :], block[...], right[term])

    add_terms(info, slots, sectors, grid, [blocks.at[place] for place in range(count)], left, right, add)
    sent[...] = total[...].astype(jnp.bfloat16)


def far_rest_kernel(slots, sectors, grid, count, info, blocks, left, right, before, sent, kept, total):
    me = lax.axis_index("term")
    partner = me + 1 - 2 * lax.rem(me, 2)
    own_shards, share = kept.shape[0], kept.shape[1]
    total[...] = before[...]

    def add(term, block):
        total[...] += product(left[term], block[...], right[term])

    add_terms(info, slots, sectors, grid, [blocks.at[place] for place in range(count)], left, right, add)
    sent[...] = total[shard_rows(partner, share), :].astype(jnp.bfloat16)
    for k in range(own_shards):
        kept[k] = total[shard_rows(lax.rem(me + 2 * k, 2 * own_shards), share), :]


def pass_kernel(kept, got, *sent):
    for k, part in enumerate(sent):
        part[...] = (kept[k + 1] + got[k].astype(jnp.float32)).astype(jnp.bfloat16)


def last_kernel(info, kept, *refs):
    got, out = refs[:-1], refs[-1]
    total = kept[0]
    for part in got:
        total = total + part[...].astype(jnp.float32)
    share = total.shape[0]
    row = lax.axis_index("term") * share + lax.broadcasted_iota(jnp.int32, total.shape, 0)
    out[0] = jnp.where(row < info[info.shape[0] - 1], total, 0.0).astype(jnp.bfloat16)


def call(kernel, name, shapes, in_specs, scratch, *args, out_specs=None):
    return pl.pallas_call(
        kernel,
        out_shape=[jax.ShapeDtypeStruct(shape, dtype) for shape, dtype in shapes],
        in_specs=in_specs,
        out_specs=out_specs or [VMEM] * len(shapes),
        scratch_shapes=scratch,
        compiler_params=LIMIT,
        name=name,
    )(*args)


def per_device(wave_blocks, sector_rows, term_class, left_env, right_env):
    pad, columns = wave_blocks.shape[1:]
    terms = term_class.shape[0]
    sectors, parts = lax.axis_size("sector"), lax.axis_size("term")
    grid = max(2, sectors // 4)
    share = pad // parts
    shared = 9 * pad // 512 * 16
    passed = parts // 2 - 1
    down, up = neighbour_moves(sectors, grid)
    near_slots, far_slots = {1: 0, 2: len(down) - 1}, {3: 0, 4: len(up) - 1}
    count = len(up)
    send = lambda array, pairs: lax.ppermute(array, "sector", pairs)
    swap = [(i, i ^ 1) for i in range(parts)]
    in_hbm = lambda array: pltpu.with_memory_space_constraint(array, pltpu.HBM)
    bf16, f32 = jnp.bfloat16, jnp.float32

    info, masked, first, rest = call(
        functools.partial(mask_kernel, shared),
        "mask",
        [((terms + 1,), jnp.int32), ((1, pad, columns), bf16), ((shared, columns), bf16), ((pad - 2 * shared, columns), bf16)],
        [HBM, SMEM, HBM],
        [pltpu.SMEM((terms,), jnp.int32), pltpu.SemaphoreType.DMA((2,))],
        in_hbm(term_class), sector_rows, in_hbm(wave_blocks),
        out_specs=[SMEM] + [VMEM] * 3,
    )
    firsts = [send(first, pairs) for pairs in up]
    near_blocks = [send(masked, pairs) for pairs in down]
    rests = [send(rest, pairs) for pairs in up]
    total, *env = call(
        own_kernel,
        "own_terms",
        [((pad, pad), f32), ((terms, pad, pad), bf16), ((terms, pad, pad), bf16)],
        [SMEM, VMEM, HBM, HBM],
        [pltpu.SemaphoreType.DMA((2, terms))],
        info, masked, in_hbm(left_env), in_hbm(right_env),
    )
    firsts, total = lax.optimization_barrier((firsts, total))
    swapped = [lax.ppermute(array, "term", swap) for array in firsts]
    (total,) = call(
        functools.partial(near_kernel, near_slots, sectors, grid),
        "near_terms",
        [((pad, pad), f32)],
        [SMEM] + [VMEM] * (len(down) + 3),
        [],
        info, *near_blocks, *env, total,
    )
    sent, blocks = call(
        functools.partial(far_first_kernel, far_slots, sectors, grid, count),
        "far_first",
        [((passed, share, pad), bf16), ((count, pad, columns), bf16)],
        [SMEM] + [VMEM] * (3 * count + 3),
        [pltpu.VMEM((passed, share, pad), f32)],
        info, *firsts, *swapped, *rests, *env, total,
    )
    got = lax.ppermute(sent, "term", swap)
    sent, kept = call(
        functools.partial(far_rest_kernel, far_slots, sectors, grid, count),
        "far_rest",
        [((share, pad), bf16), ((passed + 1, share, pad), f32)],
        [SMEM] + [VMEM] * 4,
        [pltpu.VMEM((pad, pad), f32)],
        info, blocks, *env, total,
    )
    last = [lax.ppermute(sent, "term", swap)]
    sums = call(
        pass_kernel,
        "pass_on",
        [((share, pad), bf16)] * passed,
        [VMEM] * 2,
        [],
        kept, got,
    )
    for k, part in enumerate(sums, 1):
        last.append(lax.ppermute(part, "term", [(i, (i + 2 * k) % parts) for i in range(parts)]))
    (out,) = call(
        last_kernel,
        "sum_parts",
        [((1, share, pad), bf16)],
        [SMEM] + [VMEM] * (1 + len(last)),
        [],
        info, kept, *last,
    )
    return out


def solution(mesh):
    placed = (
        P(("groups", "sector"), None, None),
        P(("groups", "sector")),
        P(("groups", "term")),
        P(("groups", "term"), "sector", None, None),
        P(("groups", "term"), "sector", None, None),
    )
    return jax.shard_map(
        per_device,
        mesh=mesh,
        in_specs=placed,
        out_specs=P(("groups", "sector"), "term", None),
        check_vma=False,
    )
```

```python
import functools

import jax
import jax.numpy as jnp
from jax import lax
from jax.experimental import pallas as pl
from jax.experimental.pallas import tpu as pltpu
from jax.sharding import PartitionSpec as P

SMEM = pl.BlockSpec(memory_space=pltpu.SMEM)
VMEM = pl.BlockSpec(memory_space=pltpu.VMEM)
HBM = pl.BlockSpec(memory_space=pltpu.HBM)
LIMIT = pltpu.CompilerParams(vmem_limit_bytes=24 * 2**20)


def neighbour_moves(sectors, grid):
    down_in = [(s, s + 1) for s in range(sectors - 1) if (s + 1) % grid != 0]
    down_out = [(s, s - 1) for s in range(1, sectors) if s % grid != 0]
    up_in = [(s, s + grid) for s in range(sectors - grid)]
    up_out = [(s, s - grid) for s in range(grid, sectors)]
    moves = []
    for first, second in ((down_in, down_out), (up_in, up_out)):
        targets = [t for _, t in first + second]
        if len(set(targets)) == len(targets):
            moves.append([first + second])
        else:
            moves.append([first, second])
    return moves


def usable_of(kind, own, sectors, grid):
    column = lax.rem(own, grid)
    usable = kind == 0
    usable = usable | ((kind == 1) & (column != 0))
    usable = usable | ((kind == 2) & (column != grid - 1))
    usable = usable | ((kind == 3) & (own >= grid))
    return usable | ((kind == 4) & (own < sectors - grid))


def slot_of(kind, slots):
    member = functools.reduce(jnp.logical_or, [kind == k for k in slots])
    return member, sum(jnp.where(kind == k, place, 0) for k, place in slots.items())


def shard_rows(shard, share):
    return pl.ds(pl.multiple_of(shard * share, share), share)


def add_terms(info, slots, sectors, grid, blocks, left, right, add):
    own = lax.axis_index("sector")
    for term in range(left.shape[0]):
        member, slot = slot_of(info[term], slots)
        usable = member & usable_of(info[term], own, sectors, grid)
        for place, block in enumerate(blocks):

            @pl.when(usable & (slot == place))
            def _():
                add(term, block)


def product(left, block, right):
    half = jnp.dot(left, block, preferred_element_type=jnp.float32)
    return lax.dot_general(
        half.astype(jnp.bfloat16), right, (((1,), (1,)), ((), ())), preferred_element_type=jnp.float32
    )


def mask_rows(block, rows, start=0):
    row = start + lax.broadcasted_iota(jnp.int32, block.shape, 0)
    return jnp.where(row < rows, block, jnp.zeros((), block.dtype))


def cut_kernel(shared, wave_hbm, first, rest, sems):
    odd = lax.rem(lax.axis_index("term"), 2)
    copies = [
        pltpu.make_async_copy(wave_hbm.at[0, shard_rows(odd, shared)], first, sems.at[0]),
        pltpu.make_async_copy(wave_hbm.at[0, pl.ds(2 * shared, rest.shape[0])], rest, sems.at[1]),
    ]
    for copy in copies:
        copy.start()
    for copy in copies:
        copy.wait()


def own_kernel(classes_hbm, rows, wave_hbm, left_hbm, right_hbm, info, total, left, right, block, classes, sems):
    terms = left.shape[0]
    get_classes = pltpu.make_async_copy(classes_hbm, classes, sems.at[0, terms])
    get_block = pltpu.make_async_copy(wave_hbm.at[0], block, sems.at[1, terms])
    get_classes.start()
    get_block.start()
    copies = []
    for term in range(terms):
        pair = (
            pltpu.make_async_copy(left_hbm.at[term, 0], left.at[term], sems.at[0, term]),
            pltpu.make_async_copy(right_hbm.at[term, 0], right.at[term], sems.at[1, term]),
        )
        for copy in pair:
            copy.start()
        copies.append(pair)
    total[...] = jnp.zeros_like(total)
    get_classes.wait()
    for term in range(terms):
        info[term] = classes[term]
    get_block.wait()
    block[...] = mask_rows(block[...], rows[0])
    for term, pair in enumerate(copies):
        for copy in pair:
            copy.wait()

        @pl.when(classes[term] == 0)
        def _():
            total[...] += product(left[term], block[...], right[term])


def near_kernel(slots, sectors, grid, count, info, *refs):
    rows, got = refs[:count], refs[count : 2 * count]
    left, right, before, total, blocks = refs[2 * count :]
    for place in range(count):
        blocks[place] = mask_rows(got[place][0], rows[place][0])
    total[...] = before[...]

    def add(term, block):
        total[...] += product(left[term], block[...], right[term])

    add_terms(info, slots, sectors, grid, [blocks.at[place] for place in range(count)], left, right, add)


def far_first_kernel(slots, sectors, grid, count, info, *refs):
    rows, firsts, swapped, rests = (refs[i * count : (i + 1) * count] for i in range(4))
    left, right, before, sent, blocks, total = refs[4 * count :]
    me = lax.axis_index("term")
    odd = lax.rem(me, 2)
    partner = me + 1 - 2 * odd
    shared = firsts[0].shape[0]
    for place in range(count):
        pieces = ((odd * shared, firsts), ((1 - odd) * shared, swapped), (2 * shared, rests))
        for start, refs_of in pieces:
            piece = refs_of[place]
            rows_at = pl.ds(pl.multiple_of(start, 16), piece.shape[0])
            blocks[place, rows_at, :] = mask_rows(piece[...], rows[place][0], start)
    passed, share = total.shape[0], total.shape[1]
    shards = [shard_rows(lax.rem(partner + 2 * (k + 1), 2 * (passed + 1)), share) for k in range(passed)]
    for k in range(passed):
        total[k] = before[shards[k], :]

    def add(term, block):
        for k in range(passed):
            total[k] += product(left[term, shards[k], :], block[...], right[term])

    add_terms(info, slots, sectors, grid, [blocks.at[place] for place in range(count)], left, right, add)
    sent[...] = total[...].astype(jnp.bfloat16)


def far_rest_kernel(slots, sectors, grid, count, info, blocks, left, right, before, sent, kept, total):
    me = lax.axis_index("term")
    partner = me + 1 - 2 * lax.rem(me, 2)
    own_shards, share = kept.shape[0], kept.shape[1]
    total[...] = before[...]

    def add(term, block):
        total[...] += product(left[term], block[...], right[term])

    add_terms(info, slots, sectors, grid, [blocks.at[place] for place in range(count)], left, right, add)
    sent[...] = total[shard_rows(partner, share), :].astype(jnp.bfloat16)
    for k in range(own_shards):
        kept[k] = total[shard_rows(lax.rem(me + 2 * k, 2 * own_shards), share), :]


def pass_kernel(kept, got, *sent):
    for k, part in enumerate(sent):
        part[...] = (kept[k + 1] + got[k].astype(jnp.float32)).astype(jnp.bfloat16)


def last_kernel(rows, kept, *refs):
    got, out = refs[:-1], refs[-1]
    total = kept[0]
    for part in got:
        total = total + part[...].astype(jnp.float32)
    share = total.shape[0]
    row = lax.axis_index("term") * share + lax.broadcasted_iota(jnp.int32, total.shape, 0)
    out[0] = jnp.where(row < rows[0], total, 0.0).astype(jnp.bfloat16)


def call(kernel, name, shapes, in_specs, scratch, *args, out_specs=None):
    return pl.pallas_call(
        kernel,
        out_shape=[jax.ShapeDtypeStruct(shape, dtype) for shape, dtype in shapes],
        in_specs=in_specs,
        out_specs=out_specs or [VMEM] * len(shapes),
        scratch_shapes=scratch,
        compiler_params=LIMIT,
        name=name,
    )(*args)


def per_device(wave_blocks, sector_rows, term_class, left_env, right_env):
    pad, columns = wave_blocks.shape[1:]
    terms = term_class.shape[0]
    sectors, parts = lax.axis_size("sector"), lax.axis_size("term")
    grid = max(2, sectors // 4)
    share = pad // parts
    shared = 11 * pad // 512 * 16
    passed = parts // 2 - 1
    down, up = neighbour_moves(sectors, grid)
    near_slots, far_slots = {1: 0, 2: len(down) - 1}, {3: 0, 4: len(up) - 1}
    count = len(up)
    send = lambda array, pairs: lax.ppermute(array, "sector", pairs)
    swap = [(i, i ^ 1) for i in range(parts)]
    in_hbm = lambda array: pltpu.with_memory_space_constraint(array, pltpu.HBM)
    bf16, f32 = jnp.bfloat16, jnp.float32

    first, rest = call(
        functools.partial(cut_kernel, shared),
        "cut",
        [((shared, columns), bf16), ((pad - 2 * shared, columns), bf16)],
        [HBM],
        [pltpu.SemaphoreType.DMA((2,))],
        in_hbm(wave_blocks),
    )
    firsts = [send(first, pairs) for pairs in up]
    near_blocks = [send(wave_blocks, pairs) for pairs in down]
    near_rows = [send(sector_rows, pairs) for pairs in down]
    far_rows = [send(sector_rows, pairs) for pairs in up]
    info, total, *env = call(
        own_kernel,
        "own_terms",
        [((terms,), jnp.int32), ((pad, pad), f32), ((terms, pad, pad), bf16), ((terms, pad, pad), bf16)],
        [HBM, SMEM] + [HBM] * 3,
        [pltpu.VMEM((pad, columns), bf16), pltpu.SMEM((terms,), jnp.int32), pltpu.SemaphoreType.DMA((2, terms + 1))],
        in_hbm(term_class), sector_rows, *(in_hbm(array) for array in (wave_blocks, left_env, right_env)),
        out_specs=[SMEM] + [VMEM] * 3,
    )
    firsts, rest, total = lax.optimization_barrier((firsts, rest, total))
    swapped = [lax.ppermute(array, "term", swap) for array in firsts]
    rests = [send(rest, pairs) for pairs in up]

    (total,) = call(
        functools.partial(near_kernel, near_slots, sectors, grid, len(down)),
        "near_terms",
        [((pad, pad), f32)],
        [SMEM] * (1 + len(down)) + [VMEM] * (len(down) + 3),
        [pltpu.VMEM((len(down), pad, columns), bf16)],
        info, *near_rows, *near_blocks, *env, total,
    )
    sent, blocks = call(
        functools.partial(far_first_kernel, far_slots, sectors, grid, count),
        "far_first",
        [((passed, share, pad), bf16), ((count, pad, columns), bf16)],
        [SMEM] * (1 + count) + [VMEM] * (3 * count + 3),
        [pltpu.VMEM((passed, share, pad), f32)],
        info, *far_rows, *firsts, *swapped, *rests, *env, total,
    )
    got = lax.ppermute(sent, "term", swap)
    sent, kept = call(
        functools.partial(far_rest_kernel, far_slots, sectors, grid, count),
        "far_rest",
        [((share, pad), bf16), ((passed + 1, share, pad), f32)],
        [SMEM] + [VMEM] * 4,
        [pltpu.VMEM((pad, pad), f32)],
        info, blocks, *env, total,
    )
    sums = call(
        pass_kernel,
        "pass_on",
        [((share, pad), bf16)] * passed,
        [VMEM] * 2,
        [],
        kept, got,
    )
    last = [
        lax.ppermute(part, "term", [(i, (i + 2 * k) % parts) for i in range(parts)])
        for k, part in enumerate(sums, 1)
    ]
    sent, *sums = lax.optimization_barrier((sent, *sums))
    last.append(lax.ppermute(sent, "term", swap))
    (out,) = call(
        last_kernel,
        "sum_parts",
        [((1, share, pad), bf16)],
        [SMEM] + [VMEM] * (1 + len(last)),
        [],
        sector_rows, kept, *last,
    )
    return out


def solution(mesh):
    placed = (
        P(("groups", "sector"), None, None),
        P(("groups", "sector")),
        P(("groups", "term")),
        P(("groups", "term"), "sector", None, None),
        P(("groups", "term"), "sector", None, None),
    )
    return jax.shard_map(
        per_device,
        mesh=mesh,
        in_specs=placed,
        out_specs=P(("groups", "sector"), "term", None),
        check_vma=False,
    )
```

```python
import functools

import jax
import jax.numpy as jnp
from jax import lax
from jax.experimental import pallas as pl
from jax.experimental.pallas import tpu as pltpu
from jax.sharding import PartitionSpec as P

SMEM = pl.BlockSpec(memory_space=pltpu.SMEM)
VMEM = pl.BlockSpec(memory_space=pltpu.VMEM)
HBM = pl.BlockSpec(memory_space=pltpu.HBM)
LIMIT = pltpu.CompilerParams(vmem_limit_bytes=24 * 2**20)


def neighbour_moves(sectors, grid):
    down_in = [(s, s + 1) for s in range(sectors - 1) if (s + 1) % grid != 0]
    down_out = [(s, s - 1) for s in range(1, sectors) if s % grid != 0]
    up_in = [(s, s + grid) for s in range(sectors - grid)]
    up_out = [(s, s - grid) for s in range(grid, sectors)]
    moves = []
    for first, second in ((down_in, down_out), (up_in, up_out)):
        targets = [t for _, t in first + second]
        if len(set(targets)) == len(targets):
            moves.append([first + second])
        else:
            moves.append([first, second])
    return moves


def usable_of(kind, own, sectors, grid):
    column = lax.rem(own, grid)
    usable = kind == 0
    usable = usable | ((kind == 1) & (column != 0))
    usable = usable | ((kind == 2) & (column != grid - 1))
    usable = usable | ((kind == 3) & (own >= grid))
    return usable | ((kind == 4) & (own < sectors - grid))


def slot_of(kind, slots):
    member = functools.reduce(jnp.logical_or, [kind == k for k in slots])
    return member, sum(jnp.where(kind == k, place, 0) for k, place in slots.items())


def shard_rows(shard, share):
    return pl.ds(pl.multiple_of(shard * share, share), share)


def add_terms(info, slots, sectors, grid, blocks, left, right, add):
    own = lax.axis_index("sector")
    for term in range(left.shape[0]):
        member, slot = slot_of(info[term], slots)
        usable = member & usable_of(info[term], own, sectors, grid)
        for place, block in enumerate(blocks):

            @pl.when(usable & (slot == place))
            def _():
                add(term, block)


def product(left, block, right):
    half = jnp.dot(left, block, preferred_element_type=jnp.float32)
    return lax.dot_general(
        half.astype(jnp.bfloat16), right, (((1,), (1,)), ((), ())), preferred_element_type=jnp.float32
    )


def mask_rows(block, rows):
    row = lax.broadcasted_iota(jnp.int32, block.shape, 0)
    return jnp.where(row < rows, block, jnp.zeros((), block.dtype))


def fetch(left_hbm, right_hbm, left, right, sems):
    copies = []
    for term in range(left.shape[0]):
        copies.append(pltpu.make_async_copy(left_hbm.at[term, 0], left.at[term], sems.at[0, term]))
        copies.append(pltpu.make_async_copy(right_hbm.at[term, 0], right.at[term], sems.at[1, term]))
    for copy in copies:
        copy.start()
    return copies


def bring_kernel(wave_hbm, left_hbm, right_hbm, wave, left, right, sems):
    terms = left.shape[0]
    get_wave = pltpu.make_async_copy(wave_hbm, wave, sems.at[0, terms])
    get_wave.start()

    @pl.when(lax.rem(lax.axis_index("sector"), 2) == 1)
    def _():
        for copy in fetch(left_hbm, right_hbm, left, right, sems):
            copy.wait()

    get_wave.wait()


def near_kernel(slots, sectors, grid, count, classes_hbm, left_hbm, right_hbm, _, __, *refs):
    rows, got = refs[:count], refs[count : 2 * count]
    info, total, left, right, blocks, classes, sems = refs[2 * count :]
    terms = left.shape[0]
    get_classes = pltpu.make_async_copy(classes_hbm, classes, sems.at[0, terms])
    get_classes.start()

    @pl.when(lax.rem(lax.axis_index("sector"), 2) == 0)
    def _():
        for copy in fetch(left_hbm, right_hbm, left, right, sems):
            copy.wait()

    total[...] = jnp.zeros_like(total)
    for place in range(count):
        blocks[place] = mask_rows(got[place][0], rows[place][0])
    get_classes.wait()
    for term in range(terms):
        info[term] = classes[term]

    def add(term, block):
        total[...] += product(left[term], block[...], right[term])

    add_terms(classes, slots, sectors, grid, [blocks.at[place] for place in range(count)], left, right, add)


def far_first_kernel(slots, sectors, grid, count, info, *refs):
    rows, got = refs[:count], refs[count : 2 * count]
    left, right, before, sent, blocks, total = refs[2 * count :]
    me = lax.axis_index("term")
    partner = me + 1 - 2 * lax.rem(me, 2)
    for place in range(count):
        blocks[place] = mask_rows(got[place][0], rows[place][0])
    passed, share = total.shape[0], total.shape[1]
    shards = [shard_rows(lax.rem(partner + 2 * (k + 1), 2 * (passed + 1)), share) for k in range(passed)]
    for k in range(passed):
        total[k] = before[shards[k], :]

    def add(term, block):
        for k in range(passed):
            total[k] += product(left[term, shards[k], :], block[...], right[term])

    add_terms(info, slots, sectors, grid, [blocks.at[place] for place in range(count)], left, right, add)
    sent[...] = total[...].astype(jnp.bfloat16)


def far_rest_kernel(slots, sectors, grid, count, info, blocks, left, right, before, sent, kept, total):
    me = lax.axis_index("term")
    partner = me + 1 - 2 * lax.rem(me, 2)
    own_shards, share = kept.shape[0], kept.shape[1]
    total[...] = before[...]

    def add(term, block):
        total[...] += product(left[term], block[...], right[term])

    add_terms(info, slots, sectors, grid, [blocks.at[place] for place in range(count)], left, right, add)
    sent[...] = total[shard_rows(partner, share), :].astype(jnp.bfloat16)
    for k in range(own_shards):
        kept[k] = total[shard_rows(lax.rem(me + 2 * k, 2 * own_shards), share), :]


def pass_kernel(kept, got, *sent):
    for k, part in enumerate(sent):
        part[...] = (kept[k + 1] + got[k].astype(jnp.float32)).astype(jnp.bfloat16)


def last_kernel(rows, kept, *refs):
    got, out = refs[:-1], refs[-1]
    total = kept[0]
    for part in got:
        total = total + part[...].astype(jnp.float32)
    share = total.shape[0]
    row = lax.axis_index("term") * share + lax.broadcasted_iota(jnp.int32, total.shape, 0)
    out[0] = jnp.where(row < rows[0], total, 0.0).astype(jnp.bfloat16)


def call(kernel, name, shapes, in_specs, scratch, *args, out_specs=None, aliases=None):
    return pl.pallas_call(
        kernel,
        out_shape=[jax.ShapeDtypeStruct(shape, dtype) for shape, dtype in shapes],
        in_specs=in_specs,
        out_specs=out_specs or [VMEM] * len(shapes),
        scratch_shapes=scratch,
        input_output_aliases=aliases or {},
        compiler_params=LIMIT,
        name=name,
    )(*args)


def per_device(wave_blocks, sector_rows, term_class, left_env, right_env):
    pad, columns = wave_blocks.shape[1:]
    terms = term_class.shape[0]
    sectors, parts = lax.axis_size("sector"), lax.axis_size("term")
    grid = max(2, sectors // 4)
    share = pad // parts
    passed = parts // 2 - 1
    down, up = neighbour_moves(sectors, grid)
    near_slots, far_slots = {0: 0, 1: 1, 2: len(down)}, {3: 0, 4: len(up) - 1}
    count = len(up)
    send = lambda array, pairs: lax.ppermute(array, "sector", pairs)
    swap = [(i, i ^ 1) for i in range(parts)]
    in_hbm = lambda array: pltpu.with_memory_space_constraint(array, pltpu.HBM)
    bf16, f32 = jnp.bfloat16, jnp.float32

    env_shape = ((terms, pad, pad), bf16)
    env_hbm = (in_hbm(left_env), in_hbm(right_env))
    near_blocks = [send(wave_blocks, pairs) for pairs in down]
    near_rows = [send(sector_rows, pairs) for pairs in down]
    wave, *env = call(
        bring_kernel,
        "bring",
        [((1, pad, columns), bf16), env_shape, env_shape],
        [HBM] * 3,
        [pltpu.SemaphoreType.DMA((2, terms + 1))],
        in_hbm(wave_blocks), *env_hbm,
    )
    far_blocks = [send(wave, pairs) for pairs in up]
    far_rows = [send(sector_rows, pairs) for pairs in up]
    near_count = 1 + len(down)
    info, total, *env = call(
        functools.partial(near_kernel, near_slots, sectors, grid, near_count),
        "near_terms",
        [((terms,), jnp.int32), ((pad, pad), f32), env_shape, env_shape],
        [HBM] * 3 + [VMEM] * 2 + [SMEM] * near_count + [VMEM] * near_count,
        [
            pltpu.VMEM((near_count, pad, columns), bf16),
            pltpu.SMEM((terms,), jnp.int32),
            pltpu.SemaphoreType.DMA((2, terms + 1)),
        ],
        in_hbm(term_class), *env_hbm, *env, sector_rows, *near_rows, wave, *near_blocks,
        out_specs=[SMEM] + [VMEM] * 3,
        aliases={3: 2, 4: 3},
    )
    sent, blocks = call(
        functools.partial(far_first_kernel, far_slots, sectors, grid, count),
        "far_first",
        [((passed, share, pad), bf16), ((count, pad, columns), bf16)],
        [SMEM] * (1 + count) + [VMEM] * (count + 3),
        [pltpu.VMEM((passed, share, pad), f32)],
        info, *far_rows, *far_blocks, *env, total,
    )
    got = lax.ppermute(sent, "term", swap)
    sent, kept = call(
        functools.partial(far_rest_kernel, far_slots, sectors, grid, count),
        "far_rest",
        [((share, pad), bf16), ((passed + 1, share, pad), f32)],
        [SMEM] + [VMEM] * 4,
        [pltpu.VMEM((pad, pad), f32)],
        info, blocks, *env, total,
    )
    last = [lax.ppermute(sent, "term", swap)]
    sums = call(
        pass_kernel,
        "pass_on",
        [((share, pad), bf16)] * passed,
        [VMEM] * 2,
        [],
        kept, got,
    )
    for k, part in enumerate(sums, 1):
        last.append(lax.ppermute(part, "term", [(i, (i + 2 * k) % parts) for i in range(parts)]))
    (out,) = call(
        last_kernel,
        "sum_parts",
        [((1, share, pad), bf16)],
        [SMEM] + [VMEM] * (1 + len(last)),
        [],
        sector_rows, kept, *last,
    )
    return out


def solution(mesh):
    placed = (
        P(("groups", "sector"), None, None),
        P(("groups", "sector")),
        P(("groups", "term")),
        P(("groups", "term"), "sector", None, None),
        P(("groups", "term"), "sector", None, None),
    )
    return jax.shard_map(
        per_device,
        mesh=mesh,
        in_specs=placed,
        out_specs=P(("groups", "sector"), "term", None),
        check_vma=False,
    )
```

```python
import functools

import jax
import jax.numpy as jnp
from jax import lax
from jax.experimental import pallas as pl
from jax.experimental.pallas import tpu as pltpu
from jax.sharding import PartitionSpec as P

SMEM = pl.BlockSpec(memory_space=pltpu.SMEM)
VMEM = pl.BlockSpec(memory_space=pltpu.VMEM)
HBM = pl.BlockSpec(memory_space=pltpu.HBM)
LIMIT = pltpu.CompilerParams(vmem_limit_bytes=24 * 2**20)


def neighbour_moves(sectors, grid):
    down_in = [(s, s + 1) for s in range(sectors - 1) if (s + 1) % grid != 0]
    down_out = [(s, s - 1) for s in range(1, sectors) if s % grid != 0]
    up_in = [(s, s + grid) for s in range(sectors - grid)]
    up_out = [(s, s - grid) for s in range(grid, sectors)]
    moves = []
    for first, second in ((down_in, down_out), (up_in, up_out)):
        targets = [t for _, t in first + second]
        if len(set(targets)) == len(targets):
            moves.append([first + second])
        else:
            moves.append([first, second])
    return moves


def usable_of(kind, own, sectors, grid):
    column = lax.rem(own, grid)
    usable = kind == 0
    usable = usable | ((kind == 1) & (column != 0))
    usable = usable | ((kind == 2) & (column != grid - 1))
    usable = usable | ((kind == 3) & (own >= grid))
    return usable | ((kind == 4) & (own < sectors - grid))


def slot_of(kind, slots):
    member = functools.reduce(jnp.logical_or, [kind == k for k in slots])
    return member, sum(jnp.where(kind == k, place, 0) for k, place in slots.items())


def shard_rows(shard, share):
    return pl.ds(pl.multiple_of(shard * share, share), share)


def add_terms(info, slots, sectors, grid, blocks, left, right, add):
    own = lax.axis_index("sector")
    for term in range(left.shape[0]):
        member, slot = slot_of(info[term], slots)
        usable = member & usable_of(info[term], own, sectors, grid)
        for place, block in enumerate(blocks):

            @pl.when(usable & (slot == place))
            def _():
                add(term, block)


def product(left, block, right):
    half = jnp.dot(left, block, preferred_element_type=jnp.float32)
    return lax.dot_general(
        half.astype(jnp.bfloat16), right, (((1,), (1,)), ((), ())), preferred_element_type=jnp.float32
    )


def mask_rows(block, rows):
    row = lax.broadcasted_iota(jnp.int32, block.shape, 0)
    return jnp.where(row < rows, block, jnp.zeros((), block.dtype))


def near_kernel(slots, sectors, grid, count, classes_hbm, wave_hbm, left_hbm, right_hbm, *refs):
    rows, got = refs[:count], refs[count : 2 * count - 1]
    info, total, left, right, blocks, classes, sems = refs[2 * count - 1 :]
    terms = left.shape[0]
    get_classes = pltpu.make_async_copy(classes_hbm, classes, sems.at[0, terms])
    get_block = pltpu.make_async_copy(wave_hbm.at[0], blocks.at[0], sems.at[1, terms])
    get_classes.start()
    get_block.start()
    copies = []
    for term in range(terms):
        pair = (
            pltpu.make_async_copy(left_hbm.at[term, 0], left.at[term], sems.at[0, term]),
            pltpu.make_async_copy(right_hbm.at[term, 0], right.at[term], sems.at[1, term]),
        )
        for copy in pair:
            copy.start()
        copies.append(pair)
    total[...] = jnp.zeros_like(total)
    for place, block in enumerate(got, 1):
        blocks[place] = mask_rows(block[0], rows[place][0])
    get_classes.wait()
    for term in range(terms):
        info[term] = classes[term]
    get_block.wait()
    blocks[0] = mask_rows(blocks[0], rows[0][0])
    for pair in copies:
        for copy in pair:
            copy.wait()

    def add(term, block):
        total[...] += product(left[term], block[...], right[term])

    add_terms(classes, slots, sectors, grid, [blocks.at[place] for place in range(count)], left, right, add)


def far_first_kernel(slots, sectors, grid, count, info, *refs):
    rows, got = refs[:count], refs[count : 2 * count]
    left, right, before, sent, blocks, total = refs[2 * count :]
    me = lax.axis_index("term")
    partner = me + 1 - 2 * lax.rem(me, 2)
    for place in range(count):
        blocks[place] = mask_rows(got[place][0], rows[place][0])
    passed, share = total.shape[0], total.shape[1]
    shards = [shard_rows(lax.rem(partner + 2 * (k + 1), 2 * (passed + 1)), share) for k in range(passed)]
    for k in range(passed):
        total[k] = before[shards[k], :]

    def add(term, block):
        for k in range(passed):
            total[k] += product(left[term, shards[k], :], block[...], right[term])

    add_terms(info, slots, sectors, grid, [blocks.at[place] for place in range(count)], left, right, add)
    sent[...] = total[...].astype(jnp.bfloat16)


def far_rest_kernel(slots, sectors, grid, count, info, blocks, left, right, before, sent, kept, total):
    me = lax.axis_index("term")
    partner = me + 1 - 2 * lax.rem(me, 2)
    own_shards, share = kept.shape[0], kept.shape[1]
    total[...] = before[...]

    def add(term, block):
        total[...] += product(left[term], block[...], right[term])

    add_terms(info, slots, sectors, grid, [blocks.at[place] for place in range(count)], left, right, add)
    sent[...] = total[shard_rows(partner, share), :].astype(jnp.bfloat16)
    for k in range(own_shards):
        kept[k] = total[shard_rows(lax.rem(me + 2 * k, 2 * own_shards), share), :]


def pass_kernel(kept, got, *sent):
    for k, part in enumerate(sent):
        part[...] = (kept[k + 1] + got[k].astype(jnp.float32)).astype(jnp.bfloat16)


def last_kernel(rows, kept, *refs):
    got, out = refs[:-1], refs[-1]
    total = kept[0]
    for part in got:
        total = total + part[...].astype(jnp.float32)
    share = total.shape[0]
    row = lax.axis_index("term") * share + lax.broadcasted_iota(jnp.int32, total.shape, 0)
    out[0] = jnp.where(row < rows[0], total, 0.0).astype(jnp.bfloat16)


def call(kernel, name, shapes, in_specs, scratch, *args, out_specs=None):
    return pl.pallas_call(
        kernel,
        out_shape=[jax.ShapeDtypeStruct(shape, dtype) for shape, dtype in shapes],
        in_specs=in_specs,
        out_specs=out_specs or [VMEM] * len(shapes),
        scratch_shapes=scratch,
        compiler_params=LIMIT,
        name=name,
    )(*args)


def per_device(wave_blocks, sector_rows, term_class, left_env, right_env):
    pad, columns = wave_blocks.shape[1:]
    terms = term_class.shape[0]
    sectors, parts = lax.axis_size("sector"), lax.axis_size("term")
    grid = max(2, sectors // 4)
    share = pad // parts
    passed = parts // 2 - 1
    down, up = neighbour_moves(sectors, grid)
    near_slots, far_slots = {0: 0, 1: 1, 2: len(down)}, {3: 0, 4: len(up) - 1}
    count = len(up)
    send = lambda array, pairs: lax.ppermute(array, "sector", pairs)
    swap = [(i, i ^ 1) for i in range(parts)]
    in_hbm = lambda array: pltpu.with_memory_space_constraint(array, pltpu.HBM)
    bf16, f32 = jnp.bfloat16, jnp.float32

    far_blocks = [send(wave_blocks, pairs) for pairs in up]
    near_blocks = [send(wave_blocks, pairs) for pairs in down]
    near_rows = [sector_rows] + [send(sector_rows, pairs) for pairs in down]
    far_rows = [send(sector_rows, pairs) for pairs in up]
    near_count = len(near_rows)
    env_shape = ((terms, pad, pad), bf16)
    info, total, *env = call(
        functools.partial(near_kernel, near_slots, sectors, grid, near_count),
        "near_terms",
        [((terms,), jnp.int32), ((pad, pad), f32), env_shape, env_shape],
        [HBM] * 4 + [SMEM] * near_count + [VMEM] * len(down),
        [
            pltpu.VMEM((near_count, pad, columns), bf16),
            pltpu.SMEM((terms,), jnp.int32),
            pltpu.SemaphoreType.DMA((2, terms + 1)),
        ],
        *(in_hbm(array) for array in (term_class, wave_blocks, left_env, right_env)), *near_rows, *near_blocks,
        out_specs=[SMEM] + [VMEM] * 3,
    )
    sent, blocks = call(
        functools.partial(far_first_kernel, far_slots, sectors, grid, count),
        "far_first",
        [((passed, share, pad), bf16), ((count, pad, columns), bf16)],
        [SMEM] * (1 + count) + [VMEM] * (count + 3),
        [pltpu.VMEM((passed, share, pad), f32)],
        info, *far_rows, *far_blocks, *env, total,
    )
    got = lax.ppermute(sent, "term", swap)
    sent, kept = call(
        functools.partial(far_rest_kernel, far_slots, sectors, grid, count),
        "far_rest",
        [((share, pad), bf16), ((passed + 1, share, pad), f32)],
        [SMEM] + [VMEM] * 4,
        [pltpu.VMEM((pad, pad), f32)],
        info, blocks, *env, total,
    )
    last = [lax.ppermute(sent, "term", swap)]
    sums = call(
        pass_kernel,
        "pass_on",
        [((share, pad), bf16)] * passed,
        [VMEM] * 2,
        [],
        kept, got,
    )
    for k, part in enumerate(sums, 1):
        last.append(lax.ppermute(part, "term", [(i, (i + 2 * k) % parts) for i in range(parts)]))
    (out,) = call(
        last_kernel,
        "sum_parts",
        [((1, share, pad), bf16)],
        [SMEM] + [VMEM] * (1 + len(last)),
        [],
        sector_rows, kept, *last,
    )
    return out


def solution(mesh):
    placed = (
        P(("groups", "sector"), None, None),
        P(("groups", "sector")),
        P(("groups", "term")),
        P(("groups", "term"), "sector", None, None),
        P(("groups", "term"), "sector", None, None),
    )
    return jax.shard_map(
        per_device,
        mesh=mesh,
        in_specs=placed,
        out_specs=P(("groups", "sector"), "term", None),
        check_vma=False,
    )
```

```python
import functools

import jax
import jax.numpy as jnp
from jax import lax
from jax.experimental import pallas as pl
from jax.experimental.pallas import tpu as pltpu
from jax.sharding import PartitionSpec as P

SMEM = pl.BlockSpec(memory_space=pltpu.SMEM)
VMEM = pl.BlockSpec(memory_space=pltpu.VMEM)
HBM = pl.BlockSpec(memory_space=pltpu.HBM)
LIMIT = pltpu.CompilerParams(vmem_limit_bytes=24 * 2**20)


def neighbour_moves(sectors, grid):
    down_in = [(s, s + 1) for s in range(sectors - 1) if (s + 1) % grid != 0]
    down_out = [(s, s - 1) for s in range(1, sectors) if s % grid != 0]
    up_in = [(s, s + grid) for s in range(sectors - grid)]
    up_out = [(s, s - grid) for s in range(grid, sectors)]
    moves = []
    for first, second in ((down_in, down_out), (up_in, up_out)):
        targets = [t for _, t in first + second]
        if len(set(targets)) == len(targets):
            moves.append([first + second])
        else:
            moves.append([first, second])
    return moves


def usable_of(kind, own, sectors, grid):
    column = lax.rem(own, grid)
    usable = kind == 0
    usable = usable | ((kind == 1) & (column != 0))
    usable = usable | ((kind == 2) & (column != grid - 1))
    usable = usable | ((kind == 3) & (own >= grid))
    return usable | ((kind == 4) & (own < sectors - grid))


def slot_of(kind, slots):
    member = functools.reduce(jnp.logical_or, [kind == k for k in slots])
    return member, sum(jnp.where(kind == k, place, 0) for k, place in slots.items())


def shard_rows(shard, share):
    return pl.ds(pl.multiple_of(shard * share, share), share)


def add_terms(info, slots, sectors, grid, blocks, left, right, add):
    own = lax.axis_index("sector")
    for term in range(left.shape[0]):
        member, slot = slot_of(info[term], slots)
        usable = member & usable_of(info[term], own, sectors, grid)
        for place, block in enumerate(blocks):

            @pl.when(usable & (slot == place))
            def _():
                add(term, block)


def product(left, block, right):
    half = jnp.dot(left, block, preferred_element_type=jnp.float32)
    return lax.dot_general(
        half.astype(jnp.bfloat16), right, (((1,), (1,)), ((), ())), preferred_element_type=jnp.float32
    )


def mask_rows(block, rows, start=0):
    row = start + lax.broadcasted_iota(jnp.int32, block.shape, 0)
    return jnp.where(row < rows, block, jnp.zeros((), block.dtype))


def cut_kernel(shared, wave_hbm, first, rest, sems):
    odd = lax.rem(lax.axis_index("term"), 2)
    copies = [
        pltpu.make_async_copy(wave_hbm.at[0, shard_rows(odd, shared)], first, sems.at[0]),
        pltpu.make_async_copy(wave_hbm.at[0, pl.ds(2 * shared, rest.shape[0])], rest, sems.at[1]),
    ]
    for copy in copies:
        copy.start()
    for copy in copies:
        copy.wait()


def own_kernel(classes_hbm, rows, wave_hbm, left_hbm, right_hbm, info, total, left, right, block, classes, sems):
    terms = left.shape[0]
    get_classes = pltpu.make_async_copy(classes_hbm, classes, sems.at[0, terms])
    get_block = pltpu.make_async_copy(wave_hbm.at[0], block, sems.at[1, terms])
    get_classes.start()
    get_block.start()
    copies = []
    for term in range(terms):
        pair = (
            pltpu.make_async_copy(left_hbm.at[term, 0], left.at[term], sems.at[0, term]),
            pltpu.make_async_copy(right_hbm.at[term, 0], right.at[term], sems.at[1, term]),
        )
        for copy in pair:
            copy.start()
        copies.append(pair)
    total[...] = jnp.zeros_like(total)
    get_classes.wait()
    for term in range(terms):
        info[term] = classes[term]
    get_block.wait()
    block[...] = mask_rows(block[...], rows[0])
    for term, pair in enumerate(copies):
        for copy in pair:
            copy.wait()

        @pl.when(classes[term] == 0)
        def _():
            total[...] += product(left[term], block[...], right[term])


def near_kernel(slots, sectors, grid, count, info, *refs):
    rows, got = refs[:count], refs[count : 2 * count]
    left, right, before, total, blocks = refs[2 * count :]
    for place in range(count):
        blocks[place] = mask_rows(got[place][0], rows[place][0])
    total[...] = before[...]

    def add(term, block):
        total[...] += product(left[term], block[...], right[term])

    add_terms(info, slots, sectors, grid, [blocks.at[place] for place in range(count)], left, right, add)


def far_first_kernel(slots, sectors, grid, count, info, *refs):
    rows, firsts, swapped, rests = (refs[i * count : (i + 1) * count] for i in range(4))
    left, right, before, sent, blocks, total = refs[4 * count :]
    me = lax.axis_index("term")
    odd = lax.rem(me, 2)
    partner = me + 1 - 2 * odd
    shared = firsts[0].shape[0]
    for place in range(count):
        pieces = ((odd * shared, firsts), ((1 - odd) * shared, swapped), (2 * shared, rests))
        for start, refs_of in pieces:
            piece = refs_of[place]
            rows_at = pl.ds(pl.multiple_of(start, 16), piece.shape[0])
            blocks[place, rows_at, :] = mask_rows(piece[...], rows[place][0], start)
    passed, share = total.shape[0], total.shape[1]
    shards = [shard_rows(lax.rem(partner + 2 * (k + 1), 2 * (passed + 1)), share) for k in range(passed)]
    for k in range(passed):
        total[k] = before[shards[k], :]

    def add(term, block):
        for k in range(passed):
            total[k] += product(left[term, shards[k], :], block[...], right[term])

    add_terms(info, slots, sectors, grid, [blocks.at[place] for place in range(count)], left, right, add)
    sent[...] = total[...].astype(jnp.bfloat16)


def far_rest_kernel(slots, sectors, grid, count, info, blocks, left, right, before, sent, kept, total):
    me = lax.axis_index("term")
    partner = me + 1 - 2 * lax.rem(me, 2)
    own_shards, share = kept.shape[0], kept.shape[1]
    total[...] = before[...]

    def add(term, block):
        total[...] += product(left[term], block[...], right[term])

    add_terms(info, slots, sectors, grid, [blocks.at[place] for place in range(count)], left, right, add)
    sent[...] = total[shard_rows(partner, share), :].astype(jnp.bfloat16)
    for k in range(own_shards):
        kept[k] = total[shard_rows(lax.rem(me + 2 * k, 2 * own_shards), share), :]


def pass_kernel(kept, got, *sent):
    for k, part in enumerate(sent):
        part[...] = (kept[k + 1] + got[k].astype(jnp.float32)).astype(jnp.bfloat16)


def last_kernel(rows, kept, *refs):
    got, out = refs[:-1], refs[-1]
    total = kept[0]
    for part in got:
        total = total + part[...].astype(jnp.float32)
    share = total.shape[0]
    row = lax.axis_index("term") * share + lax.broadcasted_iota(jnp.int32, total.shape, 0)
    out[0] = jnp.where(row < rows[0], total, 0.0).astype(jnp.bfloat16)


def call(kernel, name, shapes, in_specs, scratch, *args, out_specs=None):
    return pl.pallas_call(
        kernel,
        out_shape=[jax.ShapeDtypeStruct(shape, dtype) for shape, dtype in shapes],
        in_specs=in_specs,
        out_specs=out_specs or [VMEM] * len(shapes),
        scratch_shapes=scratch,
        compiler_params=LIMIT,
        name=name,
    )(*args)


def per_device(wave_blocks, sector_rows, term_class, left_env, right_env):
    pad, columns = wave_blocks.shape[1:]
    terms = term_class.shape[0]
    sectors, parts = lax.axis_size("sector"), lax.axis_size("term")
    grid = max(2, sectors // 4)
    share = pad // parts
    shared = pad // 4
    passed = parts // 2 - 1
    down, up = neighbour_moves(sectors, grid)
    near_slots, far_slots = {1: 0, 2: len(down) - 1}, {3: 0, 4: len(up) - 1}
    count = len(up)
    send = lambda array, pairs: lax.ppermute(array, "sector", pairs)
    swap = [(i, i ^ 1) for i in range(parts)]
    in_hbm = lambda array: pltpu.with_memory_space_constraint(array, pltpu.HBM)
    bf16, f32 = jnp.bfloat16, jnp.float32

    first, rest = call(
        functools.partial(cut_kernel, shared),
        "cut",
        [((shared, columns), bf16), ((pad - 2 * shared, columns), bf16)],
        [HBM],
        [pltpu.SemaphoreType.DMA((2,))],
        in_hbm(wave_blocks),
    )
    firsts = [send(first, pairs) for pairs in up]
    rests = [send(rest, pairs) for pairs in up]
    near_blocks = [send(wave_blocks, pairs) for pairs in down]
    near_rows = [send(sector_rows, pairs) for pairs in down]
    far_rows = [send(sector_rows, pairs) for pairs in up]
    info, total, *env = call(
        own_kernel,
        "own_terms",
        [((terms,), jnp.int32), ((pad, pad), f32), ((terms, pad, pad), bf16), ((terms, pad, pad), bf16)],
        [HBM, SMEM] + [HBM] * 3,
        [pltpu.VMEM((pad, columns), bf16), pltpu.SMEM((terms,), jnp.int32), pltpu.SemaphoreType.DMA((2, terms + 1))],
        in_hbm(term_class), sector_rows, *(in_hbm(array) for array in (wave_blocks, left_env, right_env)),
        out_specs=[SMEM] + [VMEM] * 3,
    )
    firsts, total = lax.optimization_barrier((firsts, total))
    swapped = [lax.ppermute(array, "term", swap) for array in firsts]

    (total,) = call(
        functools.partial(near_kernel, near_slots, sectors, grid, len(down)),
        "near_terms",
        [((pad, pad), f32)],
        [SMEM] * (1 + len(down)) + [VMEM] * (len(down) + 3),
        [pltpu.VMEM((len(down), pad, columns), bf16)],
        info, *near_rows, *near_blocks, *env, total,
    )
    sent, blocks = call(
        functools.partial(far_first_kernel, far_slots, sectors, grid, count),
        "far_first",
        [((passed, share, pad), bf16), ((count, pad, columns), bf16)],
        [SMEM] * (1 + count) + [VMEM] * (3 * count + 3),
        [pltpu.VMEM((passed, share, pad), f32)],
        info, *far_rows, *firsts, *swapped, *rests, *env, total,
    )
    got = lax.ppermute(sent, "term", swap)
    sent, kept = call(
        functools.partial(far_rest_kernel, far_slots, sectors, grid, count),
        "far_rest",
        [((share, pad), bf16), ((passed + 1, share, pad), f32)],
        [SMEM] + [VMEM] * 4,
        [pltpu.VMEM((pad, pad), f32)],
        info, blocks, *env, total,
    )
    last = [lax.ppermute(sent, "term", swap)]
    sums = call(
        pass_kernel,
        "pass_on",
        [((share, pad), bf16)] * passed,
        [VMEM] * 2,
        [],
        kept, got,
    )
    for k, part in enumerate(sums, 1):
        last.append(lax.ppermute(part, "term", [(i, (i + 2 * k) % parts) for i in range(parts)]))
    (out,) = call(
        last_kernel,
        "sum_parts",
        [((1, share, pad), bf16)],
        [SMEM] + [VMEM] * (1 + len(last)),
        [],
        sector_rows, kept, *last,
    )
    return out


def solution(mesh):
    placed = (
        P(("groups", "sector"), None, None),
        P(("groups", "sector")),
        P(("groups", "term")),
        P(("groups", "term"), "sector", None, None),
        P(("groups", "term"), "sector", None, None),
    )
    return jax.shard_map(
        per_device,
        mesh=mesh,
        in_specs=placed,
        out_specs=P(("groups", "sector"), "term", None),
        check_vma=False,
    )
```

```python
import functools

import jax
import jax.numpy as jnp
from jax import lax
from jax.experimental import pallas as pl
from jax.experimental.pallas import tpu as pltpu
from jax.sharding import PartitionSpec as P

SMEM = pl.BlockSpec(memory_space=pltpu.SMEM)
VMEM = pl.BlockSpec(memory_space=pltpu.VMEM)
HBM = pl.BlockSpec(memory_space=pltpu.HBM)
LIMIT = pltpu.CompilerParams(vmem_limit_bytes=24 * 2**20)


def neighbour_moves(sectors, grid):
    down_in = [(s, s + 1) for s in range(sectors - 1) if (s + 1) % grid != 0]
    down_out = [(s, s - 1) for s in range(1, sectors) if s % grid != 0]
    up_in = [(s, s + grid) for s in range(sectors - grid)]
    up_out = [(s, s - grid) for s in range(grid, sectors)]
    moves = []
    for first, second in ((down_in, down_out), (up_in, up_out)):
        targets = [t for _, t in first + second]
        if len(set(targets)) == len(targets):
            moves.append([first + second])
        else:
            moves.append([first, second])
    return moves


def usable_of(kind, own, sectors, grid):
    column = lax.rem(own, grid)
    usable = kind == 0
    usable = usable | ((kind == 1) & (column != 0))
    usable = usable | ((kind == 2) & (column != grid - 1))
    usable = usable | ((kind == 3) & (own >= grid))
    return usable | ((kind == 4) & (own < sectors - grid))


def slot_of(kind, slots):
    member = functools.reduce(jnp.logical_or, [kind == k for k in slots])
    return member, sum(jnp.where(kind == k, place, 0) for k, place in slots.items())


def shard_rows(shard, share):
    return pl.ds(pl.multiple_of(shard * share, share), share)


def add_terms(info, slots, sectors, grid, blocks, left, right, add):
    own = lax.axis_index("sector")
    for term in range(left.shape[0]):
        member, slot = slot_of(info[term], slots)
        usable = member & usable_of(info[term], own, sectors, grid)
        for place, block in enumerate(blocks):

            @pl.when(usable & (slot == place))
            def _():
                add(term, block)


def product(left, block, right):
    half = jnp.dot(left, block, preferred_element_type=jnp.float32)
    return lax.dot_general(
        half.astype(jnp.bfloat16), right, (((1,), (1,)), ((), ())), preferred_element_type=jnp.float32
    )


def mask_rows(block, rows, start=0):
    row = start + lax.broadcasted_iota(jnp.int32, block.shape, 0)
    return jnp.where(row < rows, block, jnp.zeros((), block.dtype))


def cut_kernel(shared, wave_hbm, first, rest, sems):
    odd = lax.rem(lax.axis_index("term"), 2)
    copies = [
        pltpu.make_async_copy(wave_hbm.at[0, shard_rows(odd, shared)], first, sems.at[0]),
        pltpu.make_async_copy(wave_hbm.at[0, pl.ds(2 * shared, rest.shape[0])], rest, sems.at[1]),
    ]
    for copy in copies:
        copy.start()
    for copy in copies:
        copy.wait()


def own_kernel(classes_hbm, rows, wave_hbm, left_hbm, right_hbm, info, total, left, right, block, classes, sems):
    terms = left.shape[0]
    get_classes = pltpu.make_async_copy(classes_hbm, classes, sems.at[0, terms])
    get_block = pltpu.make_async_copy(wave_hbm.at[0], block, sems.at[1, terms])
    get_classes.start()
    get_block.start()
    copies = []
    for term in range(terms):
        pair = (
            pltpu.make_async_copy(left_hbm.at[term, 0], left.at[term], sems.at[0, term]),
            pltpu.make_async_copy(right_hbm.at[term, 0], right.at[term], sems.at[1, term]),
        )
        for copy in pair:
            copy.start()
        copies.append(pair)
    total[...] = jnp.zeros_like(total)
    get_classes.wait()
    for term in range(terms):
        info[term] = classes[term]
    get_block.wait()
    block[...] = mask_rows(block[...], rows[0])
    for term, pair in enumerate(copies):
        for copy in pair:
            copy.wait()

        @pl.when(classes[term] == 0)
        def _():
            total[...] += product(left[term], block[...], right[term])


def near_kernel(slots, sectors, grid, count, info, *refs):
    rows, got = refs[:count], refs[count : 2 * count]
    left, right, before, total, blocks = refs[2 * count :]
    for place in range(count):
        blocks[place] = mask_rows(got[place][0], rows[place][0])
    total[...] = before[...]

    def add(term, block):
        total[...] += product(left[term], block[...], right[term])

    add_terms(info, slots, sectors, grid, [blocks.at[place] for place in range(count)], left, right, add)


def far_kernel(slots, sectors, grid, count, info, *refs):
    rows, firsts, swapped, rests = (refs[i * count : (i + 1) * count] for i in range(4))
    left, right, before, kept = refs[4 * count : 4 * count + 4]
    sent = refs[4 * count + 4 : -2]
    blocks, total = refs[-2:]
    me = lax.axis_index("term")
    odd = lax.rem(me, 2)
    shared = firsts[0].shape[0]
    for place in range(count):
        pieces = ((odd * shared, firsts), ((1 - odd) * shared, swapped), (2 * shared, rests))
        for start, refs_of in pieces:
            piece = refs_of[place]
            rows_at = pl.ds(pl.multiple_of(start, 16), piece.shape[0])
            blocks[place, rows_at, :] = mask_rows(piece[...], rows[place][0], start)
    total[...] = before[...]

    def add(term, block):
        total[...] += product(left[term], block[...], right[term])

    add_terms(info, slots, sectors, grid, [blocks.at[place] for place in range(count)], left, right, add)
    parts, share = len(sent) + 1, kept.shape[0]
    kept[...] = total[shard_rows(me, share), :]
    for step, part in enumerate(sent, 1):
        part[...] = total[shard_rows(me ^ step, share), :].astype(jnp.bfloat16)


def half_kernel(kept, got, total):
    total[...] = kept[...] + got[...].astype(jnp.float32)


def last_kernel(rows, kept, *refs):
    got, out = refs[:-1], refs[-1]
    total = kept[...]
    for part in got:
        total = total + part[...].astype(jnp.float32)
    share = total.shape[0]
    row = lax.axis_index("term") * share + lax.broadcasted_iota(jnp.int32, total.shape, 0)
    out[0] = jnp.where(row < rows[0], total, 0.0).astype(jnp.bfloat16)


def call(kernel, name, shapes, in_specs, scratch, *args, out_specs=None):
    return pl.pallas_call(
        kernel,
        out_shape=[jax.ShapeDtypeStruct(shape, dtype) for shape, dtype in shapes],
        in_specs=in_specs,
        out_specs=out_specs or [VMEM] * len(shapes),
        scratch_shapes=scratch,
        compiler_params=LIMIT,
        name=name,
    )(*args)


def per_device(wave_blocks, sector_rows, term_class, left_env, right_env):
    pad, columns = wave_blocks.shape[1:]
    terms = term_class.shape[0]
    sectors, parts = lax.axis_size("sector"), lax.axis_size("term")
    grid = max(2, sectors // 4)
    share = pad // parts
    shared = pad // 4
    down, up = neighbour_moves(sectors, grid)
    near_slots, far_slots = {1: 0, 2: len(down) - 1}, {3: 0, 4: len(up) - 1}
    count = len(up)
    send = lambda array, pairs: lax.ppermute(array, "sector", pairs)
    swap = [(i, i ^ 1) for i in range(parts)]
    in_hbm = lambda array: pltpu.with_memory_space_constraint(array, pltpu.HBM)
    bf16, f32 = jnp.bfloat16, jnp.float32

    first, rest = call(
        functools.partial(cut_kernel, shared),
        "cut",
        [((shared, columns), bf16), ((pad - 2 * shared, columns), bf16)],
        [HBM],
        [pltpu.SemaphoreType.DMA((2,))],
        in_hbm(wave_blocks),
    )
    firsts = [send(first, pairs) for pairs in up]
    rests = [send(rest, pairs) for pairs in up]
    near_blocks = [send(wave_blocks, pairs) for pairs in down]
    near_rows = [send(sector_rows, pairs) for pairs in down]
    far_rows = [send(sector_rows, pairs) for pairs in up]
    info, total, *env = call(
        own_kernel,
        "own_terms",
        [((terms,), jnp.int32), ((pad, pad), f32), ((terms, pad, pad), bf16), ((terms, pad, pad), bf16)],
        [HBM, SMEM] + [HBM] * 3,
        [pltpu.VMEM((pad, columns), bf16), pltpu.SMEM((terms,), jnp.int32), pltpu.SemaphoreType.DMA((2, terms + 1))],
        in_hbm(term_class), sector_rows, *(in_hbm(array) for array in (wave_blocks, left_env, right_env)),
        out_specs=[SMEM] + [VMEM] * 3,
    )
    firsts, total = lax.optimization_barrier((firsts, total))
    swapped = [lax.ppermute(array, "term", swap) for array in firsts]

    (total,) = call(
        functools.partial(near_kernel, near_slots, sectors, grid, len(down)),
        "near_terms",
        [((pad, pad), f32)],
        [SMEM] * (1 + len(down)) + [VMEM] * (len(down) + 3),
        [pltpu.VMEM((len(down), pad, columns), bf16)],
        info, *near_rows, *near_blocks, *env, total,
    )
    kept, *sent = call(
        functools.partial(far_kernel, far_slots, sectors, grid, count),
        "far_terms",
        [((share, pad), f32)] + [((share, pad), bf16)] * (parts - 1),
        [SMEM] * (1 + count) + [VMEM] * (3 * count + 3),
        [pltpu.VMEM((count, pad, columns), bf16), pltpu.VMEM((pad, pad), f32)],
        info, *far_rows, *firsts, *swapped, *rests, *env, total,
    )
    turned = [
        lax.ppermute(part, "term", [(i, i ^ step) for i in range(parts)])
        for step, part in enumerate(sent, 1)
    ]
    half = turned.pop(parts // 2 - 1)
    (kept,) = call(half_kernel, "sum_half", [((share, pad), f32)], [VMEM] * 2, [], kept, half)
    (out,) = call(
        last_kernel,
        "sum_parts",
        [((1, share, pad), bf16)],
        [SMEM] + [VMEM] * (1 + len(turned)),
        [],
        sector_rows, kept, *turned,
    )
    return out


def solution(mesh):
    placed = (
        P(("groups", "sector"), None, None),
        P(("groups", "sector")),
        P(("groups", "term")),
        P(("groups", "term"), "sector", None, None),
        P(("groups", "term"), "sector", None, None),
    )
    return jax.shard_map(
        per_device,
        mesh=mesh,
        in_specs=placed,
        out_specs=P(("groups", "sector"), "term", None),
        check_vma=False,
    )
```

```python
import functools

import jax
import jax.numpy as jnp
from jax import lax
from jax.experimental import pallas as pl
from jax.experimental.pallas import tpu as pltpu
from jax.sharding import PartitionSpec as P

SMEM = pl.BlockSpec(memory_space=pltpu.SMEM)
VMEM = pl.BlockSpec(memory_space=pltpu.VMEM)
HBM = pl.BlockSpec(memory_space=pltpu.HBM)
LIMIT = pltpu.CompilerParams(vmem_limit_bytes=24 * 2**20)


def neighbour_moves(sectors, grid):
    down_in = [(s, s + 1) for s in range(sectors - 1) if (s + 1) % grid != 0]
    down_out = [(s, s - 1) for s in range(1, sectors) if s % grid != 0]
    up_in = [(s, s + grid) for s in range(sectors - grid)]
    up_out = [(s, s - grid) for s in range(grid, sectors)]
    moves = []
    for first, second in ((down_in, down_out), (up_in, up_out)):
        targets = [t for _, t in first + second]
        if len(set(targets)) == len(targets):
            moves.append([first + second])
        else:
            moves.append([first, second])
    return moves


def usable_of(kind, own, sectors, grid):
    column = lax.rem(own, grid)
    usable = kind == 0
    usable = usable | ((kind == 1) & (column != 0))
    usable = usable | ((kind == 2) & (column != grid - 1))
    usable = usable | ((kind == 3) & (own >= grid))
    return usable | ((kind == 4) & (own < sectors - grid))


def slot_of(kind, slots):
    member = functools.reduce(jnp.logical_or, [kind == k for k in slots])
    return member, sum(jnp.where(kind == k, place, 0) for k, place in slots.items())


def shard_rows(shard, share):
    return pl.ds(pl.multiple_of(shard * share, share), share)


def add_terms(info, slots, sectors, grid, blocks, left, right, add):
    own = lax.axis_index("sector")
    for term in range(left.shape[0]):
        member, slot = slot_of(info[term], slots)
        usable = member & usable_of(info[term], own, sectors, grid)
        for place, block in enumerate(blocks):

            @pl.when(usable & (slot == place))
            def _():
                add(term, block)


def product(left, block, right):
    half = jnp.dot(left, block, preferred_element_type=jnp.float32)
    return lax.dot_general(
        half.astype(jnp.bfloat16), right, (((1,), (1,)), ((), ())), preferred_element_type=jnp.float32
    )


def mask_rows(block, rows, start=0):
    row = start + lax.broadcasted_iota(jnp.int32, block.shape, 0)
    return jnp.where(row < rows, block, jnp.zeros((), block.dtype))


def cut_kernel(shared, wave_hbm, first, rest, sems):
    odd = lax.rem(lax.axis_index("term"), 2)
    copies = [
        pltpu.make_async_copy(wave_hbm.at[0, shard_rows(odd, shared)], first, sems.at[0]),
        pltpu.make_async_copy(wave_hbm.at[0, pl.ds(2 * shared, rest.shape[0])], rest, sems.at[1]),
    ]
    for copy in copies:
        copy.start()
    for copy in copies:
        copy.wait()


def own_kernel(classes_hbm, rows, wave_hbm, left_hbm, right_hbm, info, total, left, right, block, classes, sems):
    terms = left.shape[0]
    get_classes = pltpu.make_async_copy(classes_hbm, classes, sems.at[0, terms])
    get_block = pltpu.make_async_copy(wave_hbm.at[0], block, sems.at[1, terms])
    get_classes.start()
    get_block.start()
    copies = []
    for term in range(terms):
        pair = (
            pltpu.make_async_copy(left_hbm.at[term, 0], left.at[term], sems.at[0, term]),
            pltpu.make_async_copy(right_hbm.at[term, 0], right.at[term], sems.at[1, term]),
        )
        for copy in pair:
            copy.start()
        copies.append(pair)
    total[...] = jnp.zeros_like(total)
    get_classes.wait()
    for term in range(terms):
        info[term] = classes[term]
    get_block.wait()
    block[...] = mask_rows(block[...], rows[0])
    for term, pair in enumerate(copies):
        for copy in pair:
            copy.wait()

        @pl.when(classes[term] == 0)
        def _():
            total[...] += product(left[term], block[...], right[term])


def near_kernel(slots, sectors, grid, count, info, *refs):
    rows, got = refs[:count], refs[count : 2 * count]
    left, right, _, total, blocks = refs[2 * count :]
    for place in range(count):
        blocks[place] = mask_rows(got[place][0], rows[place][0])

    def add(term, block):
        total[...] += product(left[term], block[...], right[term])

    add_terms(info, slots, sectors, grid, [blocks.at[place] for place in range(count)], left, right, add)


def far_kernel(slots, sectors, grid, count, info, *refs):
    rows, firsts, swapped, rests = (refs[i * count : (i + 1) * count] for i in range(4))
    left, right, _, total, kept = refs[4 * count : 4 * count + 5]
    sent = refs[4 * count + 5 : -1]
    blocks = refs[-1]
    me = lax.axis_index("term")
    odd = lax.rem(me, 2)
    shared = firsts[0].shape[0]
    for place in range(count):
        pieces = ((odd * shared, firsts), ((1 - odd) * shared, swapped), (2 * shared, rests))
        for start, refs_of in pieces:
            piece = refs_of[place]
            rows_at = pl.ds(pl.multiple_of(start, 16), piece.shape[0])
            blocks[place, rows_at, :] = mask_rows(piece[...], rows[place][0], start)

    def add(term, block):
        total[...] += product(left[term], block[...], right[term])

    add_terms(info, slots, sectors, grid, [blocks.at[place] for place in range(count)], left, right, add)
    parts, share = len(sent) + 1, kept.shape[0]
    kept[...] = total[shard_rows(me, share), :]
    for step, part in enumerate(sent, 1):
        part[...] = total[shard_rows(me ^ step, share), :].astype(jnp.bfloat16)


def half_kernel(kept, got, total):
    total[...] = kept[...] + got[...].astype(jnp.float32)


def last_kernel(rows, kept, *refs):
    got, out = refs[:-1], refs[-1]
    total = kept[...]
    for part in got:
        total = total + part[...].astype(jnp.float32)
    share = total.shape[0]
    row = lax.axis_index("term") * share + lax.broadcasted_iota(jnp.int32, total.shape, 0)
    out[0] = jnp.where(row < rows[0], total, 0.0).astype(jnp.bfloat16)


def call(kernel, name, shapes, in_specs, scratch, *args, out_specs=None, aliases=None):
    return pl.pallas_call(
        kernel,
        out_shape=[jax.ShapeDtypeStruct(shape, dtype) for shape, dtype in shapes],
        in_specs=in_specs,
        out_specs=out_specs or [VMEM] * len(shapes),
        scratch_shapes=scratch,
        input_output_aliases=aliases or {},
        compiler_params=LIMIT,
        name=name,
    )(*args)


def per_device(wave_blocks, sector_rows, term_class, left_env, right_env):
    pad, columns = wave_blocks.shape[1:]
    terms = term_class.shape[0]
    sectors, parts = lax.axis_size("sector"), lax.axis_size("term")
    grid = max(2, sectors // 4)
    share = pad // parts
    shared = pad // 4
    down, up = neighbour_moves(sectors, grid)
    near_slots, far_slots = {1: 0, 2: len(down) - 1}, {3: 0, 4: len(up) - 1}
    count = len(up)
    send = lambda array, pairs: lax.ppermute(array, "sector", pairs)
    swap = [(i, i ^ 1) for i in range(parts)]
    in_hbm = lambda array: pltpu.with_memory_space_constraint(array, pltpu.HBM)
    bf16, f32 = jnp.bfloat16, jnp.float32

    first, rest = call(
        functools.partial(cut_kernel, shared),
        "cut",
        [((shared, columns), bf16), ((pad - 2 * shared, columns), bf16)],
        [HBM],
        [pltpu.SemaphoreType.DMA((2,))],
        in_hbm(wave_blocks),
    )
    firsts = [send(first, pairs) for pairs in up]
    rests = [send(rest, pairs) for pairs in up]
    near_blocks = [send(wave_blocks, pairs) for pairs in down]
    near_rows = [send(sector_rows, pairs) for pairs in down]
    far_rows = [send(sector_rows, pairs) for pairs in up]
    info, total, *env = call(
        own_kernel,
        "own_terms",
        [((terms,), jnp.int32), ((pad, pad), f32), ((terms, pad, pad), bf16), ((terms, pad, pad), bf16)],
        [HBM, SMEM] + [HBM] * 3,
        [pltpu.VMEM((pad, columns), bf16), pltpu.SMEM((terms,), jnp.int32), pltpu.SemaphoreType.DMA((2, terms + 1))],
        in_hbm(term_class), sector_rows, *(in_hbm(array) for array in (wave_blocks, left_env, right_env)),
        out_specs=[SMEM] + [VMEM] * 3,
    )
    firsts, total = lax.optimization_barrier((firsts, total))
    swapped = [lax.ppermute(array, "term", swap) for array in firsts]

    (total,) = call(
        functools.partial(near_kernel, near_slots, sectors, grid, len(down)),
        "near_terms",
        [((pad, pad), f32)],
        [SMEM] * (1 + len(down)) + [VMEM] * (len(down) + 3),
        [pltpu.VMEM((len(down), pad, columns), bf16)],
        info, *near_rows, *near_blocks, *env, total,
        aliases={3 + 2 * len(down): 0},
    )
    _, kept, *sent = call(
        functools.partial(far_kernel, far_slots, sectors, grid, count),
        "far_terms",
        [((pad, pad), f32), ((share, pad), f32)] + [((share, pad), bf16)] * (parts - 1),
        [SMEM] * (1 + count) + [VMEM] * (3 * count + 3),
        [pltpu.VMEM((count, pad, columns), bf16)],
        info, *far_rows, *firsts, *swapped, *rests, *env, total,
        aliases={3 + 4 * count: 0},
    )
    turned = [
        lax.ppermute(part, "term", [(i, i ^ step) for i in range(parts)])
        for step, part in enumerate(sent, 1)
    ]
    half = turned.pop(parts // 2 - 1)
    (kept,) = call(half_kernel, "sum_half", [((share, pad), f32)], [VMEM] * 2, [], kept, half)
    (out,) = call(
        last_kernel,
        "sum_parts",
        [((1, share, pad), bf16)],
        [SMEM] + [VMEM] * (1 + len(turned)),
        [],
        sector_rows, kept, *turned,
    )
    return out


def solution(mesh):
    placed = (
        P(("groups", "sector"), None, None),
        P(("groups", "sector")),
        P(("groups", "term")),
        P(("groups", "term"), "sector", None, None),
        P(("groups", "term"), "sector", None, None),
    )
    return jax.shard_map(
        per_device,
        mesh=mesh,
        in_specs=placed,
        out_specs=P(("groups", "sector"), "term", None),
        check_vma=False,
    )
```

```python
import functools

import jax
import jax.numpy as jnp
from jax import lax
from jax.experimental import pallas as pl
from jax.experimental.pallas import tpu as pltpu
from jax.sharding import PartitionSpec as P

SMEM = pl.BlockSpec(memory_space=pltpu.SMEM)
VMEM = pl.BlockSpec(memory_space=pltpu.VMEM)
HBM = pl.BlockSpec(memory_space=pltpu.HBM)
LIMIT = pltpu.CompilerParams(vmem_limit_bytes=24 * 2**20)


def neighbour_moves(sectors, grid):
    down_in = [(s, s + 1) for s in range(sectors - 1) if (s + 1) % grid != 0]
    down_out = [(s, s - 1) for s in range(1, sectors) if s % grid != 0]
    up_in = [(s, s + grid) for s in range(sectors - grid)]
    up_out = [(s, s - grid) for s in range(grid, sectors)]
    moves = []
    for first, second in ((down_in, down_out), (up_in, up_out)):
        targets = [t for _, t in first + second]
        if len(set(targets)) == len(targets):
            moves.append([first + second])
        else:
            moves.append([first, second])
    return moves


def usable_of(kind, own, sectors, grid):
    column = lax.rem(own, grid)
    usable = kind == 0
    usable = usable | ((kind == 1) & (column != 0))
    usable = usable | ((kind == 2) & (column != grid - 1))
    usable = usable | ((kind == 3) & (own >= grid))
    return usable | ((kind == 4) & (own < sectors - grid))


def slot_of(kind, slots):
    member = functools.reduce(jnp.logical_or, [kind == k for k in slots])
    return member, sum(jnp.where(kind == k, place, 0) for k, place in slots.items())


def shard_rows(shard, share):
    return pl.ds(pl.multiple_of(shard * share, share), share)


def add_terms(info, slots, sectors, grid, blocks, left, right, add):
    own = lax.axis_index("sector")
    for term in range(left.shape[0]):
        member, slot = slot_of(info[term], slots)
        usable = member & usable_of(info[term], own, sectors, grid)
        for place, block in enumerate(blocks):

            @pl.when(usable & (slot == place))
            def _():
                add(term, block)


def product(left, block, right):
    half = jnp.dot(left, block, preferred_element_type=jnp.float32)
    return lax.dot_general(
        half.astype(jnp.bfloat16), right, (((1,), (1,)), ((), ())), preferred_element_type=jnp.float32
    )


def mask_rows(block, rows, start=0):
    row = start + lax.broadcasted_iota(jnp.int32, block.shape, 0)
    return jnp.where(row < rows, block, jnp.zeros((), block.dtype))


def cut_kernel(shared, wave_hbm, first, rest, sems):
    odd = lax.rem(lax.axis_index("term"), 2)
    copies = [
        pltpu.make_async_copy(wave_hbm.at[0, shard_rows(odd, shared)], first, sems.at[0]),
        pltpu.make_async_copy(wave_hbm.at[0, pl.ds(2 * shared, rest.shape[0])], rest, sems.at[1]),
    ]
    for copy in copies:
        copy.start()
    for copy in copies:
        copy.wait()


def own_kernel(classes_hbm, rows, wave_hbm, left_hbm, right_hbm, info, total, left, right, block, classes, sems):
    terms = left.shape[0]
    get_classes = pltpu.make_async_copy(classes_hbm, classes, sems.at[0, terms])
    get_block = pltpu.make_async_copy(wave_hbm.at[0], block, sems.at[1, terms])
    get_classes.start()
    get_block.start()
    copies = []
    for term in range(terms):
        pair = (
            pltpu.make_async_copy(left_hbm.at[term, 0], left.at[term], sems.at[0, term]),
            pltpu.make_async_copy(right_hbm.at[term, 0], right.at[term], sems.at[1, term]),
        )
        for copy in pair:
            copy.start()
        copies.append(pair)
    total[...] = jnp.zeros_like(total)
    get_classes.wait()
    for term in range(terms):
        info[term] = classes[term]
    get_block.wait()
    block[...] = mask_rows(block[...], rows[0])
    for term, pair in enumerate(copies):
        for copy in pair:
            copy.wait()

        @pl.when(classes[term] == 0)
        def _():
            total[...] += product(left[term], block[...], right[term])


def near_kernel(slots, sectors, grid, count, info, *refs):
    rows, got = refs[:count], refs[count : 2 * count]
    left, right, before, total, blocks = refs[2 * count :]
    for place in range(count):
        blocks[place] = mask_rows(got[place][0], rows[place][0])
    total[...] = before[...]

    def add(term, block):
        total[...] += product(left[term], block[...], right[term])

    add_terms(info, slots, sectors, grid, [blocks.at[place] for place in range(count)], left, right, add)


def far_kernel(slots, sectors, grid, count, info, *refs):
    rows, firsts, swapped, rests = (refs[i * count : (i + 1) * count] for i in range(4))
    left, right, before, kept = refs[4 * count : 4 * count + 4]
    sent = refs[4 * count + 4 : -2]
    blocks, total = refs[-2:]
    me = lax.axis_index("term")
    odd = lax.rem(me, 2)
    shared = firsts[0].shape[0]
    for place in range(count):
        pieces = ((odd * shared, firsts), ((1 - odd) * shared, swapped), (2 * shared, rests))
        for start, refs_of in pieces:
            piece = refs_of[place]
            rows_at = pl.ds(pl.multiple_of(start, 16), piece.shape[0])
            blocks[place, rows_at, :] = mask_rows(piece[...], rows[place][0], start)
    total[...] = before[...]

    def add(term, block):
        total[...] += product(left[term], block[...], right[term])

    add_terms(info, slots, sectors, grid, [blocks.at[place] for place in range(count)], left, right, add)
    parts, share = len(sent) + 1, kept.shape[0]
    kept[...] = total[shard_rows(me, share), :]
    for step, part in enumerate(sent, 1):
        part[...] = total[shard_rows(lax.rem(me + step, parts), share), :].astype(jnp.bfloat16)


def half_kernel(kept, got, total):
    total[...] = kept[...] + got[...].astype(jnp.float32)


def last_kernel(rows, kept, *refs):
    got, out = refs[:-1], refs[-1]
    total = kept[...]
    for part in got:
        total = total + part[...].astype(jnp.float32)
    share = total.shape[0]
    row = lax.axis_index("term") * share + lax.broadcasted_iota(jnp.int32, total.shape, 0)
    out[0] = jnp.where(row < rows[0], total, 0.0).astype(jnp.bfloat16)


def call(kernel, name, shapes, in_specs, scratch, *args, out_specs=None):
    return pl.pallas_call(
        kernel,
        out_shape=[jax.ShapeDtypeStruct(shape, dtype) for shape, dtype in shapes],
        in_specs=in_specs,
        out_specs=out_specs or [VMEM] * len(shapes),
        scratch_shapes=scratch,
        compiler_params=LIMIT,
        name=name,
    )(*args)


def per_device(wave_blocks, sector_rows, term_class, left_env, right_env):
    pad, columns = wave_blocks.shape[1:]
    terms = term_class.shape[0]
    sectors, parts = lax.axis_size("sector"), lax.axis_size("term")
    grid = max(2, sectors // 4)
    share = pad // parts
    shared = pad // 4
    down, up = neighbour_moves(sectors, grid)
    near_slots, far_slots = {1: 0, 2: len(down) - 1}, {3: 0, 4: len(up) - 1}
    count = len(up)
    send = lambda array, pairs: lax.ppermute(array, "sector", pairs)
    swap = [(i, i ^ 1) for i in range(parts)]
    in_hbm = lambda array: pltpu.with_memory_space_constraint(array, pltpu.HBM)
    bf16, f32 = jnp.bfloat16, jnp.float32

    first, rest = call(
        functools.partial(cut_kernel, shared),
        "cut",
        [((shared, columns), bf16), ((pad - 2 * shared, columns), bf16)],
        [HBM],
        [pltpu.SemaphoreType.DMA((2,))],
        in_hbm(wave_blocks),
    )
    firsts = [send(first, pairs) for pairs in up]
    rests = [send(rest, pairs) for pairs in up]
    near_blocks = [send(wave_blocks, pairs) for pairs in down]
    near_rows = [send(sector_rows, pairs) for pairs in down]
    far_rows = [send(sector_rows, pairs) for pairs in up]
    info, total, *env = call(
        own_kernel,
        "own_terms",
        [((terms,), jnp.int32), ((pad, pad), f32), ((terms, pad, pad), bf16), ((terms, pad, pad), bf16)],
        [HBM, SMEM] + [HBM] * 3,
        [pltpu.VMEM((pad, columns), bf16), pltpu.SMEM((terms,), jnp.int32), pltpu.SemaphoreType.DMA((2, terms + 1))],
        in_hbm(term_class), sector_rows, *(in_hbm(array) for array in (wave_blocks, left_env, right_env)),
        out_specs=[SMEM] + [VMEM] * 3,
    )
    firsts, total = lax.optimization_barrier((firsts, total))
    swapped = [lax.ppermute(array, "term", swap) for array in firsts]

    (total,) = call(
        functools.partial(near_kernel, near_slots, sectors, grid, len(down)),
        "near_terms",
        [((pad, pad), f32)],
        [SMEM] * (1 + len(down)) + [VMEM] * (len(down) + 3),
        [pltpu.VMEM((len(down), pad, columns), bf16)],
        info, *near_rows, *near_blocks, *env, total,
    )
    kept, *sent = call(
        functools.partial(far_kernel, far_slots, sectors, grid, count),
        "far_terms",
        [((share, pad), f32)] + [((share, pad), bf16)] * (parts - 1),
        [SMEM] * (1 + count) + [VMEM] * (3 * count + 3),
        [pltpu.VMEM((count, pad, columns), bf16), pltpu.VMEM((pad, pad), f32)],
        info, *far_rows, *firsts, *swapped, *rests, *env, total,
    )
    turned = [
        lax.ppermute(part, "term", [(i, (i + step) % parts) for i in range(parts)])
        for step, part in enumerate(sent, 1)
    ]
    half = turned.pop(parts // 2 - 1)
    (kept,) = call(half_kernel, "sum_half", [((share, pad), f32)], [VMEM] * 2, [], kept, half)
    (out,) = call(
        last_kernel,
        "sum_parts",
        [((1, share, pad), bf16)],
        [SMEM] + [VMEM] * (1 + len(turned)),
        [],
        sector_rows, kept, *turned,
    )
    return out


def solution(mesh):
    placed = (
        P(("groups", "sector"), None, None),
        P(("groups", "sector")),
        P(("groups", "term")),
        P(("groups", "term"), "sector", None, None),
        P(("groups", "term"), "sector", None, None),
    )
    return jax.shard_map(
        per_device,
        mesh=mesh,
        in_specs=placed,
        out_specs=P(("groups", "sector"), "term", None),
        check_vma=False,
    )
```
